32 devices in a mesh: grp: 2 (over y), col: 8 (over z, x), sub: 2 (over core).
Axes of the slice: x: 2, y: 2, z: 4, core: 2. Of those that a mesh axis runs over, the one named last changes fastest.
Arguments:
- features: bfloat16 [1024, 131072], P('col', 'grp'), parts along dimension 1, may hold values from -6 to 6
- block_nodes: int32 [16, 2, 32], P('grp', 'sub'), parts along dimension 0, may hold values from 0 to 65535
- hop_two: int32 [16, 2, 10, 32], P('grp', 'sub'), parts along dimension 0, may hold values from 0 to 65535
- hop_two_count: int32 [16, 2, 32], P('grp', 'sub'), parts along dimension 0, may hold values from 1 to 10
- hop_one: int32 [16, 2, 25, 1], P(('grp', 'col'), 'sub'), parts along dimension 0, may hold values from 0 to 31
- hop_one_count: int32 [16, 2, 1], P(('grp', 'col'), 'sub'), parts along dimension 0, may hold values from 1 to 25
- labels: int32 [16, 2, 1, 112], P(('grp', 'col'), 'sub'), parts along dimension 0, may hold values 0 or 1
- weight_one: bfloat16 [2, 1024, 256], P(None, 'col'), may hold values from -0.125 to 0.125
- weight_two: bfloat16 [2, 256, 256], replicated, may hold values from -0.25 to 0.25
- weight_three: bfloat16 [256, 112], replicated, may hold values from -0.375 to 0.375
Outputs:
- hidden_one: bfloat16 [16, 2, 32, 256], P(('grp', 'col'), 'sub'), parts along dimension 0
- batch_loss: float32 [16, 2], P(('grp', 'col'), 'sub'), parts along dimension 0
- grad_weight_one: float32 [4, 1024, 256], P('grp', 'col'), parts along dimension 0
- grad_weight_two: float32 [4, 256, 256], P('grp'), parts along dimension 0
- grad_weight_three: float32 [512, 112], P('grp'), parts along dimension 0
The draws below stay inside these ranges and needn't reach their ends.
There are 2 independent parts, one for each index of `grp`. The reference program is written for one: setup_inputs(seed, part) draws one part's arguments, and reference() takes and returns one part's arrays. A program takes and returns all parts, laid end to end along the dimension named above; an argument that names none is the same for every part. Nothing has to cross between parts.
Inputs may be any that keep to these rules, and one draw needn't show every extreme that they name: `hop_one`: rows of the same batch's block.
All inputs are finite; a program needn't handle non-finite values. No bound on the sum of `labels` on one device may be relied on, other than what follows from the above.
Results may differ from the reference program's by a relative error of at most 0.007.
Values may be sent and summed in bfloat16 or wider, within the bound.
No kernel may reach another device: no remote copies, remote signals or barrier semaphores. Data moves between devices by JAX's collectives and lax.ppermute only.
A program may use at most 128 MiB of HBM per device.

```python
import jax
import jax.numpy as jnp
from jax import lax

FEAT = 1024
HID = 256
LABELS = 112
NODES = 65536
SEEDS = 1
FAN_ONE = 25
FAN_TWO = 10
BLOCK = 32
N_COL = 8
N_SUB = 2


def with_ends(drawn, own_key, low, high):
    shape = drawn.shape
    place = [jax.random.randint(jax.random.fold_in(own_key, axis), (), 0, shape[axis]) for axis in range(len(shape))]
    drawn = drawn.at[tuple(place)].set(low)
    longest = shape.index(max(shape))
    place[longest] = (place[longest] + 1) % shape[longest]
    return drawn.at[tuple(place)].set(high)


def level_of(rng, dims, shards, smallest, largest):
    loudness = 1.0
    for dim, parts in shards:
        draws = jax.random.uniform(jax.random.fold_in(jax.random.fold_in(rng, 6), dim), (parts,), jnp.float32, smallest / len(shards), largest / len(shards))
        loudness = loudness * jnp.repeat(jnp.exp(draws), dims[dim] // parts).reshape((-1,) + (1,) * (len(dims) - 1 - dim))
    return loudness


def bell_draw(rng, extent, spread, most, pieces=(), held_as=jnp.bfloat16):
    array = jax.random.normal(rng, extent, jnp.float32) * spread
    if len(pieces) > 0:
        array = level_of(rng, extent, pieces, -0.22, 0.18) * array
    return jnp.clip(array, min=-most, max=most).astype(held_as)


def setup_inputs(seed: int = 0, part: int = 0) -> dict:
    keys = jax.random.split(jax.random.key(seed), 11)
    own_keys = jax.random.split(jax.random.fold_in(keys[10], part), 11)
    features = bell_draw(own_keys[0], (FEAT, NODES), 1.0, 6.0, ((0, 8),))
    block_nodes = with_ends(jax.random.randint(own_keys[1], (N_COL, N_SUB, BLOCK), 0, NODES), jax.random.fold_in(own_keys[1], 1), 0, NODES - 1).astype(jnp.int32)
    hop_two = with_ends(jax.random.randint(own_keys[2], (N_COL, N_SUB, FAN_TWO, BLOCK), 0, NODES), jax.random.fold_in(own_keys[2], 1), 0, NODES - 1).astype(jnp.int32)
    hop_two_count = with_ends(jax.random.randint(own_keys[3], (N_COL, N_SUB, BLOCK), 1, FAN_TWO + 1), jax.random.fold_in(own_keys[3], 1), 1, FAN_TWO).astype(jnp.int32)
    hop_one = with_ends(jax.random.randint(own_keys[4], (N_COL, N_SUB, FAN_ONE, SEEDS), 0, BLOCK), jax.random.fold_in(own_keys[4], 1), 0, BLOCK - 1).astype(jnp.int32)
    hop_one_count = with_ends(jax.random.randint(own_keys[5], (N_COL, N_SUB, SEEDS), 1, FAN_ONE + 1), jax.random.fold_in(own_keys[5], 1), 1, FAN_ONE).astype(jnp.int32)
    labels = with_ends((jax.random.randint(own_keys[6], (N_COL, N_SUB, SEEDS, LABELS), 0, 3) < 1).astype(jnp.int32), jax.random.fold_in(own_keys[6], 1), 0, 1)
    weight_one = bell_draw(keys[7], (2, FEAT, HID), (2 * FEAT) ** -0.5, 0.125, ((1, 8),))
    weight_two = bell_draw(keys[8], (2, HID, HID), (2 * HID) ** -0.5, 0.25)
    weight_three = bell_draw(keys[9], (HID, LABELS), HID ** -0.5, 0.375)
    return {"features": features, "block_nodes": block_nodes, "hop_two": hop_two, "hop_two_count": hop_two_count, "hop_one": hop_one, "hop_one_count": hop_one_count, "labels": labels, "weight_one": weight_one, "weight_two": weight_two, "weight_three": weight_three}


def layer_inputs(features, nodes, neighbours, counts):
    own_rows = jnp.take(features, nodes, axis=1)
    gathered = jnp.take(features, neighbours, axis=1)
    usable = jnp.arange(FAN_TWO, dtype=jnp.int32)[:, None] < counts[None, :]
    summed = jnp.sum(jnp.where(usable[None], gathered.astype(jnp.float32), 0.0), axis=1)
    mean_part = (summed / counts.astype(jnp.float32)[None, :]).astype(jnp.bfloat16)
    return jnp.stack([own_rows, mean_part])


def silu_slope(value):
    sig = jax.nn.sigmoid(value)
    return sig * (1.0 + value * (1.0 - sig))


def reference(features, block_nodes, hop_two, hop_two_count, hop_one, hop_one_count, labels, weight_one, weight_two, weight_three):
    total_batches = N_COL * N_SUB
    nodes_all = block_nodes.reshape(total_batches, BLOCK)
    second_all = hop_two.reshape(total_batches, FAN_TWO, BLOCK)
    second_count = hop_two_count.reshape(total_batches, BLOCK)
    first_all = hop_one.reshape(total_batches, FAN_ONE, SEEDS)
    first_count = hop_one_count.reshape(total_batches, SEEDS)
    label_all = labels.reshape(total_batches, SEEDS, LABELS)

    def one_batch(carry, batch_items):
        grad_one, grad_two, grad_three = carry
        nodes, neighbours, counts, chosen, chosen_count, label_rows = batch_items
        stacked = layer_inputs(features, nodes, neighbours, counts)
        pre_one = jnp.einsum("kfr,kfh->rh", stacked.astype(jnp.float32), weight_one.astype(jnp.float32))
        hidden = (pre_one * jax.nn.sigmoid(pre_one)).astype(jnp.bfloat16)
        usable = jnp.arange(FAN_ONE, dtype=jnp.int32)[:, None] < chosen_count[None, :]
        match = chosen[:, :, None] == jnp.arange(BLOCK, dtype=jnp.int32)[None, None, :]
        adjacency = jnp.sum((match & usable[:, :, None]).astype(jnp.float32), axis=0)
        seed_count = chosen_count.astype(jnp.float32)[:, None]
        mean_two = (jnp.dot(adjacency, hidden.astype(jnp.float32)) / seed_count).astype(jnp.bfloat16)
        seed_rows = hidden[:SEEDS]
        pre_two = jnp.dot(seed_rows, weight_two[0], preferred_element_type=jnp.float32) + jnp.dot(mean_two, weight_two[1], preferred_element_type=jnp.float32)
        hidden_two = (pre_two * jax.nn.sigmoid(pre_two)).astype(jnp.bfloat16)
        logits = jnp.dot(hidden_two, weight_three, preferred_element_type=jnp.float32)
        target = label_rows.astype(jnp.float32)
        mean_loss = jnp.mean(jax.nn.softplus(logits) - target * logits)
        grad_logits = ((jax.nn.sigmoid(logits) - target) / SEEDS).astype(jnp.bfloat16)
        grad_three = grad_three + jnp.dot(hidden_two.T, grad_logits, preferred_element_type=jnp.float32)
        back_two = jnp.dot(grad_logits, weight_three.T, preferred_element_type=jnp.float32)
        grad_pre_two = (back_two * silu_slope(pre_two)).astype(jnp.bfloat16)
        grad_two = grad_two + jnp.stack([jnp.dot(seed_rows.T, grad_pre_two, preferred_element_type=jnp.float32), jnp.dot(mean_two.T, grad_pre_two, preferred_element_type=jnp.float32)])
        to_seeds = jnp.dot(grad_pre_two, weight_two[0].T, preferred_element_type=jnp.float32)
        to_means = jnp.dot(grad_pre_two, weight_two[1].T, preferred_element_type=jnp.float32) / seed_count
        grad_hidden = jnp.dot(adjacency.T, to_means, precision=lax.Precision.HIGHEST)
        grad_hidden = grad_hidden + jnp.concatenate([to_seeds, jnp.zeros((BLOCK - SEEDS, HID), jnp.float32)], axis=0)
        grad_pre_one = (grad_hidden * silu_slope(pre_one)).astype(jnp.bfloat16)
        grad_one = grad_one + jnp.einsum("kfr,rh->kfh", stacked.astype(jnp.float32), grad_pre_one.astype(jnp.float32))
        return (grad_one, grad_two, grad_three), (hidden, mean_loss)

    start_carry = (jnp.zeros((2, FEAT, HID), jnp.float32), jnp.zeros((2, HID, HID), jnp.float32), jnp.zeros((HID, LABELS), jnp.float32))
    finals, outputs = lax.scan(one_batch, start_carry, (nodes_all, second_all, second_count, first_all, first_count, label_all))
    hidden_all, losses = outputs
    return (hidden_all.reshape(N_COL, N_SUB, BLOCK, HID), losses.reshape(N_COL, N_SUB), finals[0], finals[1], finals[2])
```

```python
import functools

import jax
import jax.numpy as jnp
from jax import lax
from jax.experimental import pallas as pl
from jax.experimental.pallas import tpu as pltpu
from jax.sharding import PartitionSpec as P

BF = jnp.bfloat16
F32 = jnp.float32
VMEM = pl.BlockSpec(memory_space=pltpu.VMEM)
SMEM = pl.BlockSpec(memory_space=pltpu.SMEM)
ANY = pl.BlockSpec(memory_space=pl.ANY)
NN = (((1,), (0,)), ((), ()))
NT = (((1,), (1,)), ((), ()))
TN = (((0,), (0,)), ((), ()))


def dot(a, b, dims=NN, **kw):
    return lax.dot_general(a, b, dims, preferred_element_type=F32, **kw)


def silu_slope(value, sig):
    return sig * (1.0 + value * (1.0 - sig))


def gather_kernel(
    chunks, slots, block, unroll, ids, counts, weights, meta, features, own_ref, mean_ref, pre_ref,
    stage, rows_f32, sums, sems,
):
    nodes = features.shape[1]
    span = nodes // chunks
    depth = features.shape[0]
    count_rows = own_ref.shape[0]
    per_row = ids.shape[0] // count_rows

    def fetch(k, slot):
        return pltpu.make_async_copy(
            features.at[:, pl.ds(pl.multiple_of(k * span, span), span)], stage.at[slot], sems.at[slot]
        )

    for k in range(slots):
        fetch(k, k).start()
    rows_f32[pl.ds(nodes, 8), :] = jnp.zeros((8, depth), F32)

    def chunk(k, carry):
        slot = lax.rem(k, slots)
        fetch(k, slot).wait()

        def turn(i, carry):
            for u in range(unroll):
                at = pl.multiple_of((i * unroll + u) * block, block)
                part = stage[slot, :, pl.ds(at, block)]
                if depth % 128 == 0:
                    flipped = part.T.astype(F32)
                else:
                    flipped = part.astype(F32).T
                rows_f32[pl.ds(pl.multiple_of(k * span + at, block), block), :] = flipped
            return carry

        lax.fori_loop(0, span // block // unroll, turn, 0)

        @pl.when(k + slots < chunks)
        def _():
            fetch(k + slots, slot).start()

        return carry

    lax.fori_loop(0, chunks, chunk, 0)

    def take(g, carry):
        for q in range(8):
            base = (g * 8 + q) * per_row
            sums[g, 0, q : q + 1, :] = rows_f32[pl.ds(ids[base], 1), :]
            total = rows_f32[pl.ds(ids[base + 1], 1), :]
            for j in range(2, per_row):
                total = total + rows_f32[pl.ds(ids[base + j], 1), :]
            sums[g, 1, q : q + 1, :] = total
        return carry

    lax.fori_loop(0, count_rows // 8, take, 0)
    own = sums[:, 0].reshape(count_rows, depth).astype(BF)
    mean = (sums[:, 1].reshape(count_rows, depth) / counts[...]).astype(BF)
    own_ref[...] = own
    mean_ref[...] = mean
    pre_ref[:count_rows, :] = (dot(own, weights[0]) + dot(mean, weights[1])).astype(BF)
    pre_ref[count_rows:, :] = meta[...]


def upper_kernel(
    block_rows, labels_at, mine, theirs, w_two, w_three, hidden_ref, loss_ref, pack_ref
):
    rows = hidden_ref.shape[0]
    batches = rows // block_rows
    label_count = w_three.shape[1]
    pre_one = mine[:rows, :].astype(F32) + theirs[:rows, :].astype(F32)
    meta = (mine[rows:, :].astype(F32) + theirs[rows:, :].astype(F32))[:batches]
    sig_one = jax.nn.sigmoid(pre_one)
    hidden = (pre_one * sig_one).astype(BF)
    hidden_ref[...] = hidden
    counts = meta[:, block_rows : block_rows + 1]
    target = meta[:, labels_at : labels_at + label_count]
    batch = lax.broadcasted_iota(jnp.int32, (batches, rows), 0)
    row = lax.broadcasted_iota(jnp.int32, (batches, rows), 1)
    tiled = jnp.concatenate([meta[:, :block_rows]] * batches, axis=1)
    adjacency = jnp.where(row // block_rows == batch, tiled, 0.0)
    first = jnp.where(row == batch * block_rows, 1.0, 0.0)
    seeds = dot(first.astype(BF), hidden).astype(BF)
    mean_two = (dot(adjacency.astype(BF), hidden) / counts).astype(BF)
    pre_two = dot(seeds, w_two[0]) + dot(mean_two, w_two[1])
    sig_two = jax.nn.sigmoid(pre_two)
    hidden_two = (pre_two * sig_two).astype(BF)
    logits = dot(hidden_two, w_three[...])
    soft = jnp.maximum(logits, 0.0) + jnp.log1p(jnp.exp(-jnp.abs(logits)))
    loss_ref[...] = jnp.mean(soft - target * logits, axis=1, keepdims=True)
    grad_logits = (jax.nn.sigmoid(logits) - target).astype(BF)
    back_two = dot(grad_logits, w_three[...], NT)
    grad_two = (back_two * silu_slope(pre_two, sig_two)).astype(BF)
    to_seeds = dot(grad_two, w_two[0], NT)
    to_means = dot(grad_two, w_two[1], NT) / counts
    grad_hidden = lax.dot_general(
        jnp.concatenate([adjacency, first], axis=0),
        jnp.concatenate([to_means, to_seeds], axis=0),
        TN,
        precision=lax.Precision.HIGHEST,
        preferred_element_type=F32,
    )
    pack_ref[:rows, :] = (grad_hidden * silu_slope(pre_one, sig_one)).astype(BF)
    width = hidden.shape[1]
    blank = jnp.zeros((batches, width - label_count), F32)
    tail = jnp.concatenate(
        [
            seeds.astype(F32),
            mean_two.astype(F32),
            grad_two.astype(F32),
            hidden_two.astype(F32),
            jnp.concatenate([grad_logits.astype(F32), blank], axis=1),
            jnp.zeros((batches, width), F32),
        ],
        axis=0,
    )
    pack_ref[rows:, :] = tail.astype(BF)


def final_kernel(
    batches, label_count, own_a, mean_a, pack_a, own_b, mean_b, pack_b, one_ref, two_ref, three_ref
):
    rows = own_a.shape[0]

    def part(pack, k):
        at = rows + k * batches
        if batches % 16 == 0:
            return pack[at : at + batches, :]
        return pack[rows:, :].astype(F32)[k * batches : (k + 1) * batches].astype(BF)

    grad_a, grad_b = pack_a[:rows, :], pack_b[:rows, :]
    one_ref[0] = dot(own_a[...], grad_a, TN) + dot(own_b[...], grad_b, TN)
    one_ref[1] = dot(mean_a[...], grad_a, TN) + dot(mean_b[...], grad_b, TN)
    for k in range(2):
        two_ref[k] = dot(part(pack_a, k), part(pack_a, 2), TN) + dot(part(pack_b, k), part(pack_b, 2), TN)
    three = dot(part(pack_a, 3), part(pack_a, 4), TN) + dot(part(pack_b, 3), part(pack_b, 4), TN)
    three_ref[...] = three[:, :label_count]


def per_device(
    features,
    block_nodes,
    hop_two,
    hop_two_count,
    hop_one,
    hop_one_count,
    labels,
    weight_one,
    weight_two,
    weight_three,
):
    groups = lax.axis_size("col")
    me = lax.axis_index("col")
    depth, nodes = features.shape
    width = weight_one.shape[2]
    block_rows = block_nodes.shape[2]
    slot_count = hop_two.shape[2]
    label_count = weight_three.shape[1]
    rows = groups * block_rows

    counts = hop_two_count.reshape(groups, block_rows)
    usable = jnp.arange(slot_count, dtype=jnp.int32)[None, :, None] < counts[:, None, :]
    neighbours = jnp.where(usable, hop_two[:, 0], nodes)
    ids = jnp.concatenate([block_nodes, neighbours], axis=1)
    ids = jnp.transpose(ids, (0, 2, 1)).reshape(rows * (slot_count + 1))

    fan_first = hop_one.shape[2]
    usable_one = jnp.arange(fan_first, dtype=jnp.int32) < hop_one_count[0, 0, 0]
    match = hop_one[0, 0] == jnp.arange(block_rows, dtype=jnp.int32)[None, :]
    adjacency = jnp.sum((match & usable_one[:, None]).astype(F32), axis=0)
    labels_at = width // 2
    mine = jnp.concatenate(
        [
            adjacency,
            hop_one_count[0, 0].astype(F32),
            jnp.zeros((labels_at - block_rows - 1,), F32),
            labels[0, 0, 0].astype(F32),
            jnp.zeros((width - labels_at - label_count,), F32),
        ]
    )
    meta_rows = -(-groups // 16) * 16
    slot = jnp.arange(meta_rows, dtype=jnp.int32)[:, None] == me
    meta = jnp.where(slot, mine[None, :], 0.0).astype(BF)

    chunks = 16
    own, mean, pre = pl.pallas_call(
        functools.partial(gather_kernel, chunks, 8, 256, 16),
        out_shape=(
            jax.ShapeDtypeStruct((rows, depth), BF),
            jax.ShapeDtypeStruct((rows, depth), BF),
            jax.ShapeDtypeStruct((rows + meta_rows, width), BF),
        ),
        in_specs=[SMEM, VMEM, VMEM, VMEM, ANY],
        out_specs=(VMEM, VMEM, VMEM),
        scratch_shapes=[
            pltpu.VMEM((8, depth, nodes // chunks), BF),
            pltpu.VMEM((nodes + 8, depth), F32),
            pltpu.VMEM((rows // 8, 2, 8, depth), F32),
            pltpu.SemaphoreType.DMA((8,)),
        ],
        compiler_params=pltpu.CompilerParams(vmem_limit_bytes=56 * 2**20),
    )(ids, counts.reshape(rows, 1).astype(F32), weight_one, meta, features)

    swap = [(0, 1), (1, 0)]
    own_b = lax.ppermute(own, "sub", swap)
    mean_b = lax.ppermute(mean, "sub", swap)
    bit = 1
    while bit < groups:
        other = lax.ppermute(pre, "col", [(i, i ^ bit) for i in range(groups)])
        bit *= 2
        if bit < groups:
            pre = (pre.astype(F32) + other.astype(F32)).astype(BF)

    hidden, loss, pack = pl.pallas_call(
        functools.partial(upper_kernel, block_rows, labels_at),
        out_shape=(
            jax.ShapeDtypeStruct((rows, width), BF),
            jax.ShapeDtypeStruct((groups, 1), F32),
            jax.ShapeDtypeStruct((rows + 6 * groups, width), BF),
        ),
        in_specs=[VMEM] * 4,
        out_specs=(VMEM, VMEM, VMEM),
        compiler_params=pltpu.CompilerParams(vmem_limit_bytes=56 * 2**20),
    )(pre, other, weight_two, weight_three)

    pack_b = lax.ppermute(pack, "sub", swap)
    grad_one, grad_two, grad_three = pl.pallas_call(
        functools.partial(final_kernel, groups, label_count),
        out_shape=(
            jax.ShapeDtypeStruct((2, depth, width), F32),
            jax.ShapeDtypeStruct((2, width, width), F32),
            jax.ShapeDtypeStruct((width, label_count), F32),
        ),
        in_specs=[VMEM] * 6,
        out_specs=(VMEM, VMEM, VMEM),
        compiler_params=pltpu.CompilerParams(vmem_limit_bytes=56 * 2**20),
    )(own, mean, pack, own_b, mean_b, pack_b)
    return (
        lax.dynamic_slice_in_dim(hidden, me * block_rows, block_rows, 0).reshape(1, 1, block_rows, width),
        lax.dynamic_slice_in_dim(loss, me, 1, 0),
        grad_one,
        grad_two,
        grad_three,
    )


def solution(mesh):
    return jax.shard_map(
        per_device,
        mesh=mesh,
        in_specs=(
            P("col", "grp"),
            P("grp", "sub", None),
            P("grp", "sub", None, None),
            P("grp", "sub", None),
            P(("grp", "col"), "sub", None, None),
            P(("grp", "col"), "sub", None),
            P(("grp", "col"), "sub", None, None),
            P(None, "col", None),
            P(),
            P(),
        ),
        out_specs=(
            P(("grp", "col"), "sub", None, None),
            P(("grp", "col"), "sub"),
            P("grp", "col", None),
            P("grp", None, None),
            P("grp", None),
        ),
        check_vma=False,
    )
```

```python
import functools

import jax
import jax.numpy as jnp
from jax import lax
from jax.experimental import pallas as pl
from jax.experimental.pallas import tpu as pltpu
from jax.sharding import PartitionSpec as P

BF = jnp.bfloat16
F32 = jnp.float32
VMEM = pl.BlockSpec(memory_space=pltpu.VMEM)
HBM = pl.BlockSpec(memory_space=pltpu.HBM)
SMEM = pl.BlockSpec(memory_space=pltpu.SMEM)
NN = (((1,), (0,)), ((), ()))
NT = (((1,), (1,)), ((), ()))
TN = (((0,), (0,)), ((), ()))


def dot(a, b, dims=NN, **kw):
    return lax.dot_general(a, b, dims, preferred_element_type=F32, **kw)


def add_up(terms):
    terms = [term.astype(F32) for term in terms]
    while len(terms) > 1:
        terms = [a + b for a, b in zip(terms[::2], terms[1::2])]
    return terms[0]


def phases(groups):
    bits = groups.bit_length() - 1
    plan = []
    if bits % 2:
        bits -= 1
        plan.append([(1 << bits) | (1 << bits >> 1)])
    while bits:
        bits -= 2
        plan.append([1 << bits, 2 << bits, 3 << bits])
    return plan


def silu_slope(value, sig):
    return sig * (1.0 + value * (1.0 - sig))


def gather_kernel(
    chunks, block, unroll, labels_at, own_ids, hop_ids, hop_counts, seed_hops, labels, weights, features,
    seed_count, parts_ref, pre_ref, stage, rows_f32, sums, own_s, hop_v, hop_s, count_v, seed_s, labels_v, weights_v,
    sems, small,
):
    depth, nodes = features.shape
    span = nodes // chunks
    slots = stage.shape[0]
    groups, _, block_rows = own_ids.shape
    fan = hop_ids.shape[1]
    rows = groups * block_rows
    width = weights.shape[2]

    def fetch(k, slot):
        at = pl.multiple_of(k * span, span)
        return pltpu.make_async_copy(features.at[:, pl.ds(at, span)], stage.at[slot], sems.at[slot])

    inputs = [
        pltpu.make_async_copy(source, target, small.at[k])
        for k, (source, target) in enumerate(
            (
                (hop_ids, hop_v),
                (hop_counts, count_v),
                (own_ids, own_s),
                (seed_hops, seed_s),
                (labels, labels_v),
                (weights, weights_v),
            )
        )
    ]
    inputs[0].start()
    inputs[1].start()
    for k in range(slots):
        fetch(k, k).start()
    for copy in inputs[2:]:
        copy.start()
    rows_f32[pl.ds(nodes, 8), :] = jnp.zeros((8, depth), F32)
    inputs[0].wait()
    inputs[1].wait()
    counts = count_v[...]
    slot_of = lax.broadcasted_iota(jnp.int32, hop_v.shape, 1)
    hop_v[...] = jnp.where(slot_of < counts[:, :, None, :], hop_v[...], nodes)
    to_scalars = pltpu.make_async_copy(hop_v, hop_s, small.at[len(inputs)])
    to_scalars.start()

    def chunk(k, carry):
        slot = lax.rem(k, slots)
        fetch(k, slot).wait()

        def turn(i, carry):
            for u in range(unroll):
                at = pl.multiple_of((i * unroll + u) * block, block)
                part = stage[slot, :, pl.ds(at, block)]
                if depth % 128 == 0:
                    flipped = part.T.astype(F32)
                else:
                    flipped = part.astype(F32).T
                rows_f32[pl.ds(pl.multiple_of(k * span + at, block), block), :] = flipped
            return carry

        lax.fori_loop(0, span // block // unroll, turn, 0)

        @pl.when(k + slots < chunks)
        def _():
            fetch(k + slots, slot).start()

        return carry

    lax.fori_loop(0, chunks, chunk, 0)
    for copy in inputs[2:]:
        copy.wait()
    to_scalars.wait()

    def take(b, carry):
        for r in range(block_rows):
            g, q = r // 8, r % 8
            sums[b, g, 0, q : q + 1, :] = rows_f32[pl.ds(own_s[b, 0, r], 1), :]
            total = rows_f32[pl.ds(hop_s[b, 0, 0, r], 1), :]
            for j in range(1, fan):
                total = total + rows_f32[pl.ds(hop_s[b, j, 0, r], 1), :]
            sums[b, g, 1, q : q + 1, :] = total
        return carry

    lax.fori_loop(0, groups, take, 0)
    member = lax.broadcasted_iota(jnp.int32, (rows, groups), 0) // block_rows
    member = jnp.where(member == lax.broadcasted_iota(jnp.int32, (rows, groups), 1), 1.0, 0.0).astype(BF)
    spread = dot(member, counts.astype(F32).reshape(groups, block_rows).astype(BF))
    here = lax.broadcasted_iota(jnp.int32, (rows, block_rows), 0) % block_rows
    here = here == lax.broadcasted_iota(jnp.int32, (rows, block_rows), 1)
    per_row = jnp.sum(jnp.where(here, spread, 0.0), axis=1, keepdims=True)
    own = sums[:, :, 0].reshape(rows, depth).astype(BF)
    mean = (sums[:, :, 1].reshape(rows, depth) / per_row).astype(BF)
    parts_ref[:, :depth] = own
    parts_ref[:, depth:] = mean
    pre_ref[:rows, :] = (dot(own, weights_v[0]) + dot(mean, weights_v[1])).astype(BF)

    lane = lax.broadcasted_iota(jnp.int32, (1, width), 1)
    valid = seed_count[0, 0, 0]
    marks = jnp.where(lane == block_rows, valid.astype(F32), 0.0)
    for j in range(seed_hops.shape[3]):
        marks = marks + jnp.where((lane == seed_s[0, 0, 0, j]) & (j < valid), 1.0, 0.0)
    target = labels_v[0, 0].astype(F32)
    marks = jnp.concatenate([marks[:, :labels_at], target, marks[:, labels_at + target.shape[1] :]], axis=1)
    meta_rows = pre_ref.shape[0] - rows
    slot_row = lax.broadcasted_iota(jnp.int32, (meta_rows, width), 0) == lax.axis_index("col")
    pre_ref[rows:, :] = jnp.where(slot_row, marks, 0.0).astype(BF)


def upper_kernel(
    batches, block_rows, labels_at, w_two, w_three, *refs
):
    *terms, hidden_ref, loss_ref, pack_ref, hidden_f32 = refs
    rows, width = pack_ref.shape[0] - 6 * batches, pack_ref.shape[1]
    me = lax.axis_index("col")
    label_count = w_three.shape[0]
    pre_one = add_up([term[:rows, :] for term in terms])
    meta = add_up([term[rows:, :] for term in terms])[:batches]
    sig_one = jax.nn.sigmoid(pre_one)
    hidden = (pre_one * sig_one).astype(BF)
    hidden_f32[...] = hidden.astype(F32)
    hidden_ref[...] = hidden_f32[pl.ds(pl.multiple_of(me * block_rows, block_rows), block_rows), :].astype(BF)
    counts = meta[:, block_rows : block_rows + 1]
    target = meta[:, labels_at : labels_at + label_count]
    batch = lax.broadcasted_iota(jnp.int32, (batches, rows), 0)
    row = lax.broadcasted_iota(jnp.int32, (batches, rows), 1)
    tiled = jnp.concatenate([meta[:, :block_rows]] * batches, axis=1)
    adjacency = jnp.where(row // block_rows == batch, tiled, 0.0)
    first = jnp.where(row == batch * block_rows, 1.0, 0.0)
    seeds = dot(first.astype(BF), hidden).astype(BF)
    mean_two = (dot(adjacency.astype(BF), hidden) / counts).astype(BF)
    pre_two = dot(seeds, w_two[0]) + dot(mean_two, w_two[1])
    sig_two = jax.nn.sigmoid(pre_two)
    hidden_two = (pre_two * sig_two).astype(BF)
    logits = dot(hidden_two, w_three[...], NT)
    soft = jnp.maximum(logits, 0.0) + jnp.log1p(jnp.exp(-jnp.abs(logits)))
    losses = jnp.mean(soft - target * logits, axis=1, keepdims=True)
    chosen = lax.broadcasted_iota(jnp.int32, losses.shape, 0) == me
    loss_ref[...] = jnp.sum(jnp.where(chosen, losses, 0.0), axis=0, keepdims=True)
    grad_logits = (jax.nn.sigmoid(logits) - target).astype(BF)
    back_two = dot(grad_logits, w_three[...])
    grad_two = (back_two * silu_slope(pre_two, sig_two)).astype(BF)
    to_seeds = dot(grad_two, w_two[0], NT)
    to_means = dot(grad_two, w_two[1], NT) / counts
    grad_hidden = lax.dot_general(
        jnp.concatenate([adjacency, first], axis=0),
        jnp.concatenate([to_means, to_seeds], axis=0),
        TN,
        precision=lax.Precision.HIGHEST,
        preferred_element_type=F32,
    )
    pack_ref[:rows, :] = (grad_hidden * silu_slope(pre_one, sig_one)).astype(BF)
    blank = jnp.zeros((batches, width - label_count), F32)
    tail = jnp.concatenate(
        [
            seeds.astype(F32),
            mean_two.astype(F32),
            grad_two.astype(F32),
            hidden_two.astype(F32),
            jnp.concatenate([grad_logits.astype(F32), blank], axis=1),
            jnp.zeros((batches, width), F32),
        ],
        axis=0,
    )
    pack_ref[rows:, :] = tail.astype(BF)


def final_kernel(batches, parts_a, pack_a, parts_b, pack_b, one_ref, two_ref, three_ref):
    rows = parts_a.shape[0]
    depth = one_ref.shape[1]

    def part(pack, k):
        if batches % 16 == 0:
            return pack[rows + k * batches : rows + (k + 1) * batches, :]
        return pack[rows:, :].astype(F32)[k * batches : (k + 1) * batches].astype(BF)

    def both(k, m):
        return dot(part(pack_a, k), part(pack_a, m), TN) + dot(part(pack_b, k), part(pack_b, m), TN)

    one = dot(parts_a[...], pack_a[:rows, :], TN) + dot(parts_b[...], pack_b[:rows, :], TN)
    one_ref[0] = one[:depth]
    one_ref[1] = one[depth:]
    two_ref[0] = both(0, 2)
    two_ref[1] = both(1, 2)
    three_ref[...] = both(4, 3)[: three_ref.shape[0], :]


def per_device(
    features,
    block_nodes,
    hop_two,
    hop_two_count,
    hop_one,
    hop_one_count,
    labels,
    weight_one,
    weight_two,
    weight_three,
):
    groups = lax.axis_size("col")
    depth, nodes = features.shape
    width = weight_one.shape[2]
    block_rows = block_nodes.shape[2]
    fan = hop_two.shape[2]
    label_count = weight_three.shape[1]
    rows = groups * block_rows
    meta_rows = -(-groups // 16) * 16
    labels_at = width // 2
    chunks, slots = 16, 8
    mib = 2**20
    row_bytes = rows * width * 4

    parts, pre = pl.pallas_call(
        functools.partial(gather_kernel, chunks, 256, 16, labels_at),
        out_shape=(
            jax.ShapeDtypeStruct((rows, 2 * depth), BF),
            jax.ShapeDtypeStruct((rows + meta_rows, width), BF),
        ),
        in_specs=[HBM] * 7 + [SMEM],
        out_specs=(VMEM, VMEM),
        scratch_shapes=[
            pltpu.VMEM((slots, depth, nodes // chunks), BF),
            pltpu.VMEM((nodes + 8, depth), F32),
            pltpu.VMEM((groups, block_rows // 8, 2, 8, depth), F32),
            pltpu.SMEM((groups, 1, block_rows), jnp.int32),
            pltpu.VMEM((groups, fan, 1, block_rows), jnp.int32),
            pltpu.SMEM((groups, fan, 1, block_rows), jnp.int32),
            pltpu.VMEM((groups, 1, block_rows), jnp.int32),
            pltpu.SMEM((1, 1, 1, hop_one.shape[2]), jnp.int32),
            pltpu.VMEM((1, 1, 1, label_count), jnp.int32),
            pltpu.VMEM(weight_one.shape, BF),
            pltpu.SemaphoreType.DMA((slots,)),
            pltpu.SemaphoreType.DMA((8,)),
        ],
        compiler_params=pltpu.CompilerParams(vmem_limit_bytes=44 * mib + 2 * row_bytes),
    )(
        *(
            pltpu.with_memory_space_constraint(array, pltpu.HBM)
            for array in (
                block_nodes,
                jnp.transpose(hop_two, (0, 2, 1, 3)),
                hop_two_count,
                jnp.transpose(hop_one, (0, 1, 3, 2)),
                labels,
                weight_one,
                features,
            )
        ),
        hop_one_count,
    )

    swap = [(0, 1), (1, 0)]
    parts_b = lax.ppermute(parts, "sub", swap)
    terms = [pre]
    for number, masks in enumerate(phases(groups)):
        pre = add_up(terms).astype(BF) if number else pre
        terms = [pre] + [lax.ppermute(pre, "col", [(i, i ^ m) for i in range(groups)]) for m in masks]
        if number == 0:
            *terms, parts_b = lax.optimization_barrier((*terms, parts_b))

    hidden, loss, pack = pl.pallas_call(
        functools.partial(upper_kernel, groups, block_rows, labels_at),
        out_shape=(
            jax.ShapeDtypeStruct((block_rows, width), BF),
            jax.ShapeDtypeStruct((1, 1), F32),
            jax.ShapeDtypeStruct((rows + 6 * groups, width), BF),
        ),
        in_specs=[VMEM] * (len(terms) + 2),
        out_specs=(VMEM, VMEM, VMEM),
        scratch_shapes=[pltpu.VMEM((rows, width), F32)],
        compiler_params=pltpu.CompilerParams(vmem_limit_bytes=6 * mib + 8 * row_bytes),
    )(weight_two, weight_three.T, *terms)

    pack_b = lax.ppermute(pack, "sub", swap)
    grad_one, grad_two, grad_three = pl.pallas_call(
        functools.partial(final_kernel, groups),
        out_shape=(
            jax.ShapeDtypeStruct((2, depth, width), F32),
            jax.ShapeDtypeStruct((2, width, width), F32),
            jax.ShapeDtypeStruct((label_count, width), F32),
        ),
        in_specs=[VMEM] * 4,
        out_specs=(VMEM, VMEM, VMEM),
        compiler_params=pltpu.CompilerParams(vmem_limit_bytes=6 * mib + 4 * row_bytes),
    )(parts, pack, parts_b, pack_b)
    return (
        hidden.reshape(1, 1, block_rows, width),
        loss,
        grad_one,
        grad_two,
        grad_three.T,
    )


def solution(mesh):
    return jax.shard_map(
        per_device,
        mesh=mesh,
        in_specs=(
            P("col", "grp"),
            P("grp", "sub", None),
            P("grp", "sub", None, None),
            P("grp", "sub", None),
            P(("grp", "col"), "sub", None, None),
            P(("grp", "col"), "sub", None),
            P(("grp", "col"), "sub", None, None),
            P(None, "col", None),
            P(),
            P(),
        ),
        out_specs=(
            P(("grp", "col"), "sub", None, None),
            P(("grp", "col"), "sub"),
            P("grp", "col", None),
            P("grp", None, None),
            P("grp", None),
        ),
        check_vma=False,
    )
```

```python
import functools

import jax
import jax.numpy as jnp
from jax import lax
from jax.experimental import pallas as pl
from jax.experimental.pallas import tpu as pltpu
from jax.sharding import PartitionSpec as P

BF = jnp.bfloat16
F32 = jnp.float32
VMEM = pl.BlockSpec(memory_space=pltpu.VMEM)
HBM = pl.BlockSpec(memory_space=pltpu.HBM)
SMEM = pl.BlockSpec(memory_space=pltpu.SMEM)
NN = (((1,), (0,)), ((), ()))
NT = (((1,), (1,)), ((), ()))
TN = (((0,), (0,)), ((), ()))


def dot(a, b, dims=NN, **kw):
    return lax.dot_general(a, b, dims, preferred_element_type=F32, **kw)


def add_up(terms):
    terms = [term.astype(F32) for term in terms]
    while len(terms) > 1:
        terms = [a + b for a, b in zip(terms[::2], terms[1::2])]
    return terms[0]


def phases(groups):
    bits = groups.bit_length() - 1
    plan = []
    if bits % 2:
        bits -= 1
        plan.append([(1 << bits) | (1 << bits >> 1)])
    while bits:
        bits -= 2
        plan.append([1 << bits, 2 << bits, 3 << bits])
    return plan


def silu_slope(value, sig):
    return sig * (1.0 + value * (1.0 - sig))


def gather_kernel(
    chunks, block, unroll, labels_at, own_ids, hop_ids, hop_counts, seed_hops, labels, weights, features,
    seed_count, parts_ref, pre_ref, stage, rows_f32, sums, own_s, hop_v, hop_s, count_v, seed_s, labels_v, weights_v,
    sems, small,
):
    depth, nodes = features.shape
    span = nodes // chunks
    early = 5
    groups, _, block_rows = own_ids.shape
    fan = hop_ids.shape[1]
    rows = groups * block_rows
    width = weights.shape[2]

    def fetch(k):
        at = pl.multiple_of(k * span, span)
        return pltpu.make_async_copy(features.at[:, pl.ds(at, span)], stage.at[k], sems.at[k])

    inputs = [
        pltpu.make_async_copy(source, target, small.at[k])
        for k, (source, target) in enumerate(
            (
                (hop_ids, hop_v),
                (hop_counts, count_v),
                (own_ids, own_s),
                (seed_hops, seed_s),
                (labels, labels_v),
                (weights, weights_v),
            )
        )
    ]
    for copy in inputs[:-1]:
        copy.start()
    for k in range(early):
        fetch(k).start()
    inputs[-1].start()
    rows_f32[pl.ds(nodes, 8), :] = jnp.zeros((8, depth), F32)
    inputs[0].wait()
    inputs[1].wait()
    counts = count_v[...]
    slot_of = lax.broadcasted_iota(jnp.int32, hop_v.shape, 1)
    hop_v[...] = jnp.where(slot_of < counts[:, :, None, :], hop_v[...], nodes)
    to_scalars = pltpu.make_async_copy(hop_v, hop_s, small.at[len(inputs)])
    to_scalars.start()
    for k in range(early, chunks):
        fetch(k).start()

    eye = jnp.where(lax.broadcasted_iota(jnp.int32, (block, block), 0) == lax.broadcasted_iota(jnp.int32, (block, block), 1), 1.0, 0.0).astype(BF)

    def chunk(k, carry):
        fetch(k).wait()

        def turn(i, carry):
            for u in range(unroll):
                at = pl.multiple_of((i * unroll + u) * block, block)
                part = stage[k, :, pl.ds(at, block)]
                if depth % 128 == 0:
                    flipped = part.T.astype(F32) if u % 4 else dot(eye, part, NT)
                else:
                    flipped = part.astype(F32).T
                rows_f32[pl.ds(pl.multiple_of(k * span + at, block), block), :] = flipped
            return carry

        lax.fori_loop(0, span // block // unroll, turn, 0)

        return carry

    lax.fori_loop(0, chunks, chunk, 0)
    for copy in inputs[2:]:
        copy.wait()
    to_scalars.wait()

    def take(b, carry):
        for r in range(block_rows):
            g, q = r // 8, r % 8
            sums[b, g, 0, q : q + 1, :] = rows_f32[pl.ds(own_s[b, 0, r], 1), :]
            total = rows_f32[pl.ds(hop_s[b, 0, 0, r], 1), :]
            for j in range(1, fan):
                total = total + rows_f32[pl.ds(hop_s[b, j, 0, r], 1), :]
            sums[b, g, 1, q : q + 1, :] = total
        return carry

    lax.fori_loop(0, groups, take, 0, unroll=min(groups, 8))
    member = lax.broadcasted_iota(jnp.int32, (rows, groups), 0) // block_rows
    member = jnp.where(member == lax.broadcasted_iota(jnp.int32, (rows, groups), 1), 1.0, 0.0).astype(BF)
    spread = dot(member, counts.astype(F32).reshape(groups, block_rows).astype(BF))
    here = lax.broadcasted_iota(jnp.int32, (rows, block_rows), 0) % block_rows
    here = here == lax.broadcasted_iota(jnp.int32, (rows, block_rows), 1)
    per_row = jnp.sum(jnp.where(here, spread, 0.0), axis=1, keepdims=True)
    own = sums[:, :, 0].reshape(rows, depth).astype(BF)
    mean = (sums[:, :, 1].reshape(rows, depth) / per_row).astype(BF)
    parts_ref[:, :depth] = own
    parts_ref[:, depth:] = mean
    pre_ref[:rows, :] = (dot(own, weights_v[0]) + dot(mean, weights_v[1])).astype(BF)

    lane = lax.broadcasted_iota(jnp.int32, (1, width), 1)
    valid = seed_count[0, 0, 0]
    marks = jnp.where(lane == block_rows, valid.astype(F32), 0.0)
    for j in range(seed_hops.shape[3]):
        marks = marks + jnp.where((lane == seed_s[0, 0, 0, j]) & (j < valid), 1.0, 0.0)
    target = labels_v[0, 0].astype(F32)
    marks = jnp.concatenate([marks[:, :labels_at], target, marks[:, labels_at + target.shape[1] :]], axis=1)
    meta_rows = pre_ref.shape[0] - rows
    slot_row = lax.broadcasted_iota(jnp.int32, (meta_rows, width), 0) == lax.axis_index("col")
    pre_ref[rows:, :] = jnp.where(slot_row, marks, 0.0).astype(BF)


def upper_kernel(
    batches, block_rows, labels_at, w_two, w_three, *refs
):
    *terms, hidden_ref, loss_ref, pack_ref, hidden_f32 = refs
    rows, width = pack_ref.shape[0] - 6 * batches, pack_ref.shape[1]
    me = lax.axis_index("col")
    label_count = w_three.shape[0]
    pre_one = add_up([term[:rows, :] for term in terms])
    meta = add_up([term[rows:, :] for term in terms])[:batches]
    sig_one = jax.nn.sigmoid(pre_one)
    hidden = (pre_one * sig_one).astype(BF)
    hidden_f32[...] = hidden.astype(F32)
    hidden_ref[...] = hidden_f32[pl.ds(pl.multiple_of(me * block_rows, block_rows), block_rows), :].astype(BF)
    counts = meta[:, block_rows : block_rows + 1]
    target = meta[:, labels_at : labels_at + label_count]
    batch = lax.broadcasted_iota(jnp.int32, (batches, rows), 0)
    row = lax.broadcasted_iota(jnp.int32, (batches, rows), 1)
    tiled = jnp.concatenate([meta[:, :block_rows]] * batches, axis=1)
    adjacency = jnp.where(row // block_rows == batch, tiled, 0.0)
    first = jnp.where(row == batch * block_rows, 1.0, 0.0)
    pick = jnp.concatenate([first, adjacency], axis=0).astype(BF)
    picked = dot(pick, hidden)
    seeds = picked[:batches].astype(BF)
    mean_two = (picked[batches:] / counts).astype(BF)
    w_both = w_two[...].reshape(2 * width, width)
    pre_two = dot(jnp.concatenate([seeds, mean_two], axis=1), w_both)
    sig_two = jax.nn.sigmoid(pre_two)
    hidden_two = (pre_two * sig_two).astype(BF)
    logits = dot(hidden_two, w_three[...], NT)
    soft = jnp.maximum(logits, 0.0) + jnp.log1p(jnp.exp(-jnp.abs(logits)))
    losses = jnp.mean(soft - target * logits, axis=1, keepdims=True)
    chosen = lax.broadcasted_iota(jnp.int32, losses.shape, 0) == me
    loss_ref[...] = jnp.sum(jnp.where(chosen, losses, 0.0), axis=0, keepdims=True)
    grad_logits = (jax.nn.sigmoid(logits) - target).astype(BF)
    back_two = dot(grad_logits, w_three[...])
    grad_two = (back_two * silu_slope(pre_two, sig_two)).astype(BF)
    back_both = dot(grad_two, w_both, NT)
    spread = jnp.concatenate([back_both[:, :width], back_both[:, width:] / counts], axis=0)
    pieces = []
    for _ in range(3):
        pieces.append(spread.astype(BF))
        spread = spread - pieces[-1].astype(F32)
    grad_hidden = dot(jnp.concatenate([pick] * 3, axis=0), jnp.concatenate(pieces, axis=0), TN)
    pack_ref[:rows, :] = (grad_hidden * silu_slope(pre_one, sig_one)).astype(BF)
    blank = jnp.zeros((batches, width - label_count), F32)
    tail = jnp.concatenate(
        [
            seeds.astype(F32),
            mean_two.astype(F32),
            grad_two.astype(F32),
            hidden_two.astype(F32),
            jnp.concatenate([grad_logits.astype(F32), blank], axis=1),
            jnp.zeros((batches, width), F32),
        ],
        axis=0,
    )
    pack_ref[rows:, :] = tail.astype(BF)


def final_kernel(batches, parts_a, pack_a, parts_b, pack_b, one_ref, two_ref, three_ref):
    rows = parts_a.shape[0]
    depth = one_ref.shape[1]

    def part(pack, k):
        if batches % 16 == 0:
            return pack[rows + k * batches : rows + (k + 1) * batches, :]
        return pack[rows:, :].astype(F32)[k * batches : (k + 1) * batches].astype(BF)

    def both(k, m):
        return dot(part(pack_a, k), part(pack_a, m), TN) + dot(part(pack_b, k), part(pack_b, m), TN)

    one = dot(parts_a[...], pack_a[:rows, :], TN) + dot(parts_b[...], pack_b[:rows, :], TN)
    one_ref[0] = one[:depth]
    one_ref[1] = one[depth:]
    two_ref[0] = both(0, 2)
    two_ref[1] = both(1, 2)
    three_ref[...] = both(4, 3)[: three_ref.shape[0], :]


def per_device(
    features,
    block_nodes,
    hop_two,
    hop_two_count,
    hop_one,
    hop_one_count,
    labels,
    weight_one,
    weight_two,
    weight_three,
):
    groups = lax.axis_size("col")
    depth, nodes = features.shape
    width = weight_one.shape[2]
    block_rows = block_nodes.shape[2]
    fan = hop_two.shape[2]
    label_count = weight_three.shape[1]
    rows = groups * block_rows
    meta_rows = -(-groups // 16) * 16
    labels_at = width // 2
    chunks = 16
    mib = 2**20
    row_bytes = rows * width * 4

    parts, pre = pl.pallas_call(
        functools.partial(gather_kernel, chunks, 256, 16, labels_at),
        out_shape=(
            jax.ShapeDtypeStruct((rows, 2 * depth), BF),
            jax.ShapeDtypeStruct((rows + meta_rows, width), BF),
        ),
        in_specs=[HBM] * 7 + [SMEM],
        out_specs=(VMEM, VMEM),
        scratch_shapes=[
            pltpu.VMEM((chunks, depth, nodes // chunks), BF),
            pltpu.VMEM((nodes + 8, depth), F32),
            pltpu.VMEM((groups, block_rows // 8, 2, 8, depth), F32),
            pltpu.SMEM((groups, 1, block_rows), jnp.int32),
            pltpu.VMEM((groups, fan, 1, block_rows), jnp.int32),
            pltpu.SMEM((groups, fan, 1, block_rows), jnp.int32),
            pltpu.VMEM((groups, 1, block_rows), jnp.int32),
            pltpu.SMEM((1, 1, 1, hop_one.shape[2]), jnp.int32),
            pltpu.VMEM((1, 1, 1, label_count), jnp.int32),
            pltpu.VMEM(weight_one.shape, BF),
            pltpu.SemaphoreType.DMA((chunks,)),
            pltpu.SemaphoreType.DMA((8,)),
        ],
        compiler_params=pltpu.CompilerParams(vmem_limit_bytes=52 * mib + 2 * row_bytes),
    )(
        *(
            pltpu.with_memory_space_constraint(array, pltpu.HBM)
            for array in (
                block_nodes,
                jnp.transpose(hop_two, (0, 2, 1, 3)),
                hop_two_count,
                jnp.transpose(hop_one, (0, 1, 3, 2)),
                labels,
                weight_one,
                features,
            )
        ),
        hop_one_count,
    )

    swap = [(0, 1), (1, 0)]
    parts_b = lax.ppermute(parts, "sub", swap)
    terms = [pre]
    for number, masks in enumerate(phases(groups)):
        pre = add_up(terms).astype(BF) if number else pre
        terms = [pre] + [lax.ppermute(pre, "col", [(i, i ^ m) for i in range(groups)]) for m in masks]
        if number == 0:
            *terms, parts_b = lax.optimization_barrier((*terms, parts_b))

    hidden, loss, pack = pl.pallas_call(
        functools.partial(upper_kernel, groups, block_rows, labels_at),
        out_shape=(
            jax.ShapeDtypeStruct((block_rows, width), BF),
            jax.ShapeDtypeStruct((1, 1), F32),
            jax.ShapeDtypeStruct((rows + 6 * groups, width), BF),
        ),
        in_specs=[VMEM] * (len(terms) + 2),
        out_specs=(VMEM, VMEM, VMEM),
        scratch_shapes=[pltpu.VMEM((rows, width), F32)],
        compiler_params=pltpu.CompilerParams(vmem_limit_bytes=6 * mib + 8 * row_bytes),
    )(weight_two, weight_three.T, *terms)

    pack_b = lax.ppermute(pack, "sub", swap)
    grad_one, grad_two, grad_three = pl.pallas_call(
        functools.partial(final_kernel, groups),
        out_shape=(
            jax.ShapeDtypeStruct((2, depth, width), F32),
            jax.ShapeDtypeStruct((2, width, width), F32),
            jax.ShapeDtypeStruct((label_count, width), F32),
        ),
        in_specs=[VMEM] * 4,
        out_specs=(VMEM, VMEM, VMEM),
        compiler_params=pltpu.CompilerParams(vmem_limit_bytes=6 * mib + 4 * row_bytes),
    )(parts, pack, parts_b, pack_b)
    return (
        hidden.reshape(1, 1, block_rows, width),
        loss,
        grad_one,
        grad_two,
        grad_three.T,
    )


def solution(mesh):
    return jax.shard_map(
        per_device,
        mesh=mesh,
        in_specs=(
            P("col", "grp"),
            P("grp", "sub", None),
            P("grp", "sub", None, None),
            P("grp", "sub", None),
            P(("grp", "col"), "sub", None, None),
            P(("grp", "col"), "sub", None),
            P(("grp", "col"), "sub", None, None),
            P(None, "col", None),
            P(),
            P(),
        ),
        out_specs=(
            P(("grp", "col"), "sub", None, None),
            P(("grp", "col"), "sub"),
            P("grp", "col", None),
            P("grp", None, None),
            P("grp", None),
        ),
        check_vma=False,
    )
```

```python
import functools

import jax
import jax.numpy as jnp
from jax import lax
from jax.experimental import pallas as pl
from jax.experimental.pallas import tpu as pltpu
from jax.sharding import PartitionSpec as P

BF = jnp.bfloat16
F32 = jnp.float32
VMEM = pl.BlockSpec(memory_space=pltpu.VMEM)
HBM = pl.BlockSpec(memory_space=pltpu.HBM)
SMEM = pl.BlockSpec(memory_space=pltpu.SMEM)
NN = (((1,), (0,)), ((), ()))
NT = (((1,), (1,)), ((), ()))
TN = (((0,), (0,)), ((), ()))


def dot(a, b, dims=NN, **kw):
    return lax.dot_general(a, b, dims, preferred_element_type=F32, **kw)


def add_up(terms):
    terms = [term.astype(F32) for term in terms]
    while len(terms) > 1:
        terms = [a + b for a, b in zip(terms[::2], terms[1::2])]
    return terms[0]


def phases(groups):
    bits = groups.bit_length() - 1
    plan = []
    if bits % 2:
        bits -= 1
        plan.append([(1 << bits) | (1 << bits >> 1)])
    while bits:
        bits -= 2
        plan.append([1 << bits, 2 << bits, 3 << bits])
    return plan


def silu_slope(value, sig):
    return sig * (1.0 + value * (1.0 - sig))


def gather_kernel(
    chunks, block, unroll, labels_at, own_ids, hop_ids, hop_counts, seed_hops, labels, weights, features,
    seed_count, parts_ref, pre_ref, stage, rows_f32, sums, count_rows, own_s, hop_v, hop_s, count_v, seed_s, labels_v, weights_v,
    sems, small,
):
    depth, nodes = features.shape
    span = nodes // chunks
    early = 5
    groups, _, block_rows = own_ids.shape
    fan = hop_ids.shape[1]
    rows = groups * block_rows
    width = weights.shape[2]

    def fetch(k):
        at = pl.multiple_of(k * span, span)
        return pltpu.make_async_copy(features.at[:, pl.ds(at, span)], stage.at[k], sems.at[k])

    inputs = [
        pltpu.make_async_copy(source, target, small.at[k])
        for k, (source, target) in enumerate(
            (
                (hop_ids, hop_v),
                (hop_counts, count_v),
                (own_ids, own_s),
                (seed_hops, seed_s),
                (labels, labels_v),
                (weights, weights_v),
            )
        )
    ]
    for copy in inputs[:-1]:
        copy.start()
    for k in range(early):
        fetch(k).start()
    inputs[-1].start()
    rows_f32[pl.ds(nodes, 8), :] = jnp.zeros((8, depth), F32)
    inputs[0].wait()
    inputs[1].wait()
    counts = count_v[...]
    slot_of = lax.broadcasted_iota(jnp.int32, hop_v.shape, 1)
    hop_v[...] = jnp.where(slot_of < counts[:, :, None, :], hop_v[...], nodes)
    to_scalars = pltpu.make_async_copy(hop_v, hop_s, small.at[len(inputs)])
    to_scalars.start()
    for k in range(early, chunks):
        fetch(k).start()

    member = lax.broadcasted_iota(jnp.int32, (rows, groups), 0) // block_rows
    member = jnp.where(member == lax.broadcasted_iota(jnp.int32, (rows, groups), 1), 1.0, 0.0).astype(BF)
    spread = dot(member, counts.astype(F32).reshape(groups, block_rows).astype(BF))
    here = lax.broadcasted_iota(jnp.int32, (rows, block_rows), 0) % block_rows
    here = here == lax.broadcasted_iota(jnp.int32, (rows, block_rows), 1)
    per_row = jnp.sum(jnp.where(here, spread, 0.0), axis=1, keepdims=True)
    count_rows[...] = jnp.broadcast_to(per_row, count_rows.shape)
    for copy in inputs[3:5]:
        copy.wait()
    lane = lax.broadcasted_iota(jnp.int32, (1, width), 1)
    valid = seed_count[0, 0, 0]
    marks = jnp.where(lane == block_rows, valid.astype(F32), 0.0)
    for j in range(seed_hops.shape[3]):
        marks = marks + jnp.where((lane == seed_s[0, 0, 0, j]) & (j < valid), 1.0, 0.0)
    target = labels_v[0, 0].astype(F32)
    marks = jnp.concatenate([marks[:, :labels_at], target, marks[:, labels_at + target.shape[1] :]], axis=1)
    meta_rows = pre_ref.shape[0] - rows
    slot_row = lax.broadcasted_iota(jnp.int32, (meta_rows, width), 0) == lax.axis_index("col")
    pre_ref[rows:, :] = jnp.where(slot_row, marks, 0.0).astype(BF)

    eye = jnp.where(lax.broadcasted_iota(jnp.int32, (block, block), 0) == lax.broadcasted_iota(jnp.int32, (block, block), 1), 1.0, 0.0).astype(BF)

    def chunk(k, carry):
        fetch(k).wait()

        def turn(i, carry):
            for u in range(unroll):
                at = pl.multiple_of((i * unroll + u) * block, block)
                part = stage[k, :, pl.ds(at, block)]
                if depth % 128 == 0:
                    flipped = part.T.astype(F32) if u % 4 else dot(eye, part, NT)
                else:
                    flipped = part.astype(F32).T
                rows_f32[pl.ds(pl.multiple_of(k * span + at, block), block), :] = flipped
            return carry

        lax.fori_loop(0, span // block // unroll, turn, 0)

        return carry

    lax.fori_loop(0, chunks, chunk, 0)
    inputs[2].wait()
    inputs[5].wait()
    to_scalars.wait()

    w_both = weights_v[...].reshape(2 * depth, width)

    def take(first, several):
        for b in range(several):
            b = first + b
            for r in range(block_rows):
                g, q = r // 8, r % 8
                sums[b, g, 0, q : q + 1, :] = rows_f32[pl.ds(own_s[b, 0, r], 1), :]
                total = rows_f32[pl.ds(hop_s[b, 0, 0, r], 1), :]
                for j in range(1, fan):
                    total = total + rows_f32[pl.ds(hop_s[b, j, 0, r], 1), :]
                sums[b, g, 1, q : q + 1, :] = total
        size = several * block_rows
        here = pl.ds(first * block_rows, size)
        parts_ref[here, :depth] = sums[pl.ds(first, several), :, 0].reshape(size, depth).astype(BF)
        mean = sums[pl.ds(first, several), :, 1].reshape(size, depth) / count_rows[here, :]
        parts_ref[here, depth:] = mean.astype(BF)
        pre_ref[here, :] = dot(parts_ref[here, :], w_both).astype(BF)

    several = min(groups, 4)
    if groups <= 8:
        for first in range(0, groups, several):
            take(first, several)
    else:

        @pl.loop(0, groups // several)
        def _(turn):
            take(turn * several, several)


def upper_kernel(
    batches, block_rows, labels_at, w_two, w_three, *refs
):
    *terms, hidden_ref, loss_ref, pack_ref, hidden_f32 = refs
    rows, width = pack_ref.shape[0] - 6 * batches, pack_ref.shape[1]
    me = lax.axis_index("col")
    label_count = w_three.shape[0]
    pre_one = add_up([term[:rows, :] for term in terms])
    meta = add_up([term[rows:, :] for term in terms])[:batches]
    sig_one = jax.nn.sigmoid(pre_one)
    hidden = (pre_one * sig_one).astype(BF)
    hidden_f32[...] = hidden.astype(F32)
    hidden_ref[...] = hidden_f32[pl.ds(pl.multiple_of(me * block_rows, block_rows), block_rows), :].astype(BF)
    counts = meta[:, block_rows : block_rows + 1]
    target = meta[:, labels_at : labels_at + label_count]
    batch = lax.broadcasted_iota(jnp.int32, (batches, rows), 0)
    row = lax.broadcasted_iota(jnp.int32, (batches, rows), 1)
    tiled = jnp.concatenate([meta[:, :block_rows]] * batches, axis=1)
    adjacency = jnp.where(row // block_rows == batch, tiled, 0.0)
    first = jnp.where(row == batch * block_rows, 1.0, 0.0)
    pick = jnp.concatenate([first, adjacency], axis=0).astype(BF)
    picked = dot(pick, hidden)
    seeds = picked[:batches].astype(BF)
    mean_two = (picked[batches:] / counts).astype(BF)
    w_both = w_two[...].reshape(2 * width, width)
    pre_two = dot(jnp.concatenate([seeds, mean_two], axis=1), w_both)
    sig_two = jax.nn.sigmoid(pre_two)
    hidden_two = (pre_two * sig_two).astype(BF)
    logits = dot(hidden_two, w_three[...], NT)
    soft = jnp.maximum(logits, 0.0) + jnp.log1p(jnp.exp(-jnp.abs(logits)))
    losses = jnp.mean(soft - target * logits, axis=1, keepdims=True)
    chosen = lax.broadcasted_iota(jnp.int32, losses.shape, 0) == me
    loss_ref[...] = jnp.sum(jnp.where(chosen, losses, 0.0), axis=0, keepdims=True)
    grad_logits = (jax.nn.sigmoid(logits) - target).astype(BF)
    back_two = dot(grad_logits, w_three[...])
    grad_two = (back_two * silu_slope(pre_two, sig_two)).astype(BF)
    back_both = dot(grad_two, w_both, NT)
    spread = jnp.concatenate([back_both[:, :width], back_both[:, width:] / counts], axis=0)
    pieces = []
    for _ in range(3):
        pieces.append(spread.astype(BF))
        spread = spread - pieces[-1].astype(F32)
    grad_hidden = dot(jnp.concatenate([pick] * 3, axis=0), jnp.concatenate(pieces, axis=0), TN)
    pack_ref[:rows, :] = (grad_hidden * silu_slope(pre_one, sig_one)).astype(BF)
    blank = jnp.zeros((batches, width - label_count), F32)
    tail = jnp.concatenate(
        [
            seeds.astype(F32),
            mean_two.astype(F32),
            grad_two.astype(F32),
            hidden_two.astype(F32),
            jnp.concatenate([grad_logits.astype(F32), blank], axis=1),
            jnp.zeros((batches, width), F32),
        ],
        axis=0,
    )
    pack_ref[rows:, :] = tail.astype(BF)


def products(batches, parts_t, pack):
    rows = parts_t.shape[1]

    def part(k):
        if batches % 16 == 0:
            return pack[rows + k * batches : rows + (k + 1) * batches, :]
        return pack[rows:, :].astype(F32)[k * batches : (k + 1) * batches].astype(BF)

    one = dot(parts_t, pack[:rows, :])
    return one, dot(part(0), part(2), TN), dot(part(1), part(2), TN), dot(part(4), part(3), TN)


def half_kernel(batches, parts_a, pack_a, parts_b, one_ref, two_ref, three_ref, flipped_ref):
    one, seeds, means, three = products(batches, parts_a[...].T, pack_a)
    one_ref[...] = one
    two_ref[0] = seeds
    two_ref[1] = means
    three_ref[...] = three
    flipped_ref[...] = parts_b[...].T


def final_kernel(batches, flipped, pack_b, one_a, two_a, three_a, one_ref, two_ref, three_ref):
    depth = one_ref.shape[1]
    one, seeds, means, three = products(batches, flipped[...], pack_b)
    one = one_a[...] + one
    one_ref[0] = one[:depth]
    one_ref[1] = one[depth:]
    two_ref[0] = two_a[0] + seeds
    two_ref[1] = two_a[1] + means
    three_ref[...] = (three_a[...] + three)[: three_ref.shape[0], :]


def per_device(
    features,
    block_nodes,
    hop_two,
    hop_two_count,
    hop_one,
    hop_one_count,
    labels,
    weight_one,
    weight_two,
    weight_three,
):
    groups = lax.axis_size("col")
    depth, nodes = features.shape
    width = weight_one.shape[2]
    block_rows = block_nodes.shape[2]
    fan = hop_two.shape[2]
    label_count = weight_three.shape[1]
    rows = groups * block_rows
    meta_rows = -(-groups // 16) * 16
    labels_at = width // 2
    chunks = 16
    mib = 2**20
    row_bytes = rows * width * 4

    parts, pre = pl.pallas_call(
        functools.partial(gather_kernel, chunks, 256, 16, labels_at),
        out_shape=(
            jax.ShapeDtypeStruct((rows, 2 * depth), BF),
            jax.ShapeDtypeStruct((rows + meta_rows, width), BF),
        ),
        in_specs=[HBM] * 7 + [SMEM],
        out_specs=(VMEM, VMEM),
        scratch_shapes=[
            pltpu.VMEM((chunks, depth, nodes // chunks), BF),
            pltpu.VMEM((nodes + 8, depth), F32),
            pltpu.VMEM((groups, block_rows // 8, 2, 8, depth), F32),
            pltpu.VMEM((rows, depth), F32),
            pltpu.SMEM((groups, 1, block_rows), jnp.int32),
            pltpu.VMEM((groups, fan, 1, block_rows), jnp.int32),
            pltpu.SMEM((groups, fan, 1, block_rows), jnp.int32),
            pltpu.VMEM((groups, 1, block_rows), jnp.int32),
            pltpu.SMEM((1, 1, 1, hop_one.shape[2]), jnp.int32),
            pltpu.VMEM((1, 1, 1, label_count), jnp.int32),
            pltpu.VMEM(weight_one.shape, BF),
            pltpu.SemaphoreType.DMA((chunks,)),
            pltpu.SemaphoreType.DMA((8,)),
        ],
        compiler_params=pltpu.CompilerParams(vmem_limit_bytes=52 * mib + 2 * row_bytes),
    )(
        *(
            pltpu.with_memory_space_constraint(array, pltpu.HBM)
            for array in (
                block_nodes,
                jnp.transpose(hop_two, (0, 2, 1, 3)),
                hop_two_count,
                jnp.transpose(hop_one, (0, 1, 3, 2)),
                labels,
                weight_one,
                features,
            )
        ),
        hop_one_count,
    )

    swap = [(0, 1), (1, 0)]
    parts_b = lax.ppermute(parts, "sub", swap)
    terms = [pre]
    for number, masks in enumerate(phases(groups)):
        pre = add_up(terms).astype(BF) if number else pre
        terms = [pre] + [lax.ppermute(pre, "col", [(i, i ^ m) for i in range(groups)]) for m in masks]
        if number == 0:
            *terms, parts_b = lax.optimization_barrier((*terms, parts_b))

    hidden, loss, pack = pl.pallas_call(
        functools.partial(upper_kernel, groups, block_rows, labels_at),
        out_shape=(
            jax.ShapeDtypeStruct((block_rows, width), BF),
            jax.ShapeDtypeStruct((1, 1), F32),
            jax.ShapeDtypeStruct((rows + 6 * groups, width), BF),
        ),
        in_specs=[VMEM] * (len(terms) + 2),
        out_specs=(VMEM, VMEM, VMEM),
        scratch_shapes=[pltpu.VMEM((rows, width), F32)],
        compiler_params=pltpu.CompilerParams(vmem_limit_bytes=6 * mib + 8 * row_bytes),
    )(weight_two, weight_three.T, *terms)

    pack_b = lax.ppermute(pack, "sub", swap)
    one, two, three, flipped_b = pl.pallas_call(
        functools.partial(half_kernel, groups),
        out_shape=(
            jax.ShapeDtypeStruct((2 * depth, width), F32),
            jax.ShapeDtypeStruct((2, width, width), F32),
            jax.ShapeDtypeStruct((width, width), F32),
            jax.ShapeDtypeStruct((2 * depth, rows), BF),
        ),
        in_specs=[VMEM] * 3,
        out_specs=(VMEM,) * 4,
        compiler_params=pltpu.CompilerParams(vmem_limit_bytes=6 * mib + 4 * row_bytes),
    )(parts, pack, parts_b)
    grad_one, grad_two, grad_three = pl.pallas_call(
        functools.partial(final_kernel, groups),
        out_shape=(
            jax.ShapeDtypeStruct((2, depth, width), F32),
            jax.ShapeDtypeStruct((2, width, width), F32),
            jax.ShapeDtypeStruct((label_count, width), F32),
        ),
        in_specs=[VMEM] * 5,
        out_specs=(VMEM,) * 3,
        compiler_params=pltpu.CompilerParams(vmem_limit_bytes=6 * mib + 4 * row_bytes),
    )(flipped_b, pack_b, one, two, three)
    return (
        hidden.reshape(1, 1, block_rows, width),
        loss,
        grad_one,
        grad_two,
        grad_three.T,
    )


def solution(mesh):
    return jax.shard_map(
        per_device,
        mesh=mesh,
        in_specs=(
            P("col", "grp"),
            P("grp", "sub", None),
            P("grp", "sub", None, None),
            P("grp", "sub", None),
            P(("grp", "col"), "sub", None, None),
            P(("grp", "col"), "sub", None),
            P(("grp", "col"), "sub", None, None),
            P(None, "col", None),
            P(),
            P(),
        ),
        out_specs=(
            P(("grp", "col"), "sub", None, None),
            P(("grp", "col"), "sub"),
            P("grp", "col", None),
            P("grp", None, None),
            P("grp", None),
        ),
        check_vma=False,
    )
```

```python
import functools

import jax
import jax.numpy as jnp
from jax import lax
from jax.experimental import pallas as pl
from jax.experimental.pallas import tpu as pltpu
from jax.sharding import PartitionSpec as P

BF = jnp.bfloat16
F32 = jnp.float32
VMEM = pl.BlockSpec(memory_space=pltpu.VMEM)
HBM = pl.BlockSpec(memory_space=pltpu.HBM)
SMEM = pl.BlockSpec(memory_space=pltpu.SMEM)
NN = (((1,), (0,)), ((), ()))
NT = (((1,), (1,)), ((), ()))
TN = (((0,), (0,)), ((), ()))


def dot(a, b, dims=NN, **kw):
    return lax.dot_general(a, b, dims, preferred_element_type=F32, **kw)


def add_up(terms):
    terms = [term.astype(F32) for term in terms]
    while len(terms) > 1:
        terms = [a + b for a, b in zip(terms[::2], terms[1::2])]
    return terms[0]


def phases(groups):
    bits = groups.bit_length() - 1
    plan = []
    if bits % 2:
        bits -= 1
        plan.append([(1 << bits) | (1 << bits >> 1)])
    while bits:
        bits -= 2
        plan.append([1 << bits, 2 << bits, 3 << bits])
    return plan


def silu_slope(value, sig):
    return sig * (1.0 + value * (1.0 - sig))


def gather_kernel(
    chunks, block, unroll, labels_at, own_ids, hop_ids, hop_counts, seed_hops, labels, weights, features,
    seed_count, parts_ref, pre_ref, stage, rows_f32, sums, count_rows, own_s, hop_v, hop_s, count_v, seed_s, labels_v, weights_v,
    sems, small,
):
    depth, nodes = features.shape
    span = nodes // chunks
    early = 5
    groups, _, block_rows = own_ids.shape
    fan = hop_ids.shape[1]
    rows = groups * block_rows
    width = weights.shape[2]

    def fetch(k):
        at = pl.multiple_of(k * span, span)
        return pltpu.make_async_copy(features.at[:, pl.ds(at, span)], stage.at[k], sems.at[k])

    inputs = [
        pltpu.make_async_copy(source, target, small.at[k])
        for k, (source, target) in enumerate(
            (
                (hop_ids, hop_v),
                (hop_counts, count_v),
                (own_ids, own_s),
                (seed_hops, seed_s),
                (labels, labels_v),
                (weights, weights_v),
            )
        )
    ]
    for copy in inputs[:-1]:
        copy.start()
    for k in range(early):
        fetch(k).start()
    inputs[-1].start()
    rows_f32[pl.ds(nodes, 8), :] = jnp.zeros((8, depth), F32)
    inputs[0].wait()
    inputs[1].wait()
    counts = count_v[...]
    slot_of = lax.broadcasted_iota(jnp.int32, hop_v.shape, 1)
    hop_v[...] = jnp.where(slot_of < counts[:, :, None, :], hop_v[...], nodes)
    to_scalars = pltpu.make_async_copy(hop_v, hop_s, small.at[len(inputs)])
    to_scalars.start()
    for k in range(early, chunks):
        fetch(k).start()

    member = lax.broadcasted_iota(jnp.int32, (rows, groups), 0) // block_rows
    member = jnp.where(member == lax.broadcasted_iota(jnp.int32, (rows, groups), 1), 1.0, 0.0).astype(BF)
    spread = dot(member, counts.astype(F32).reshape(groups, block_rows).astype(BF))
    here = lax.broadcasted_iota(jnp.int32, (rows, block_rows), 0) % block_rows
    here = here == lax.broadcasted_iota(jnp.int32, (rows, block_rows), 1)
    per_row = jnp.sum(jnp.where(here, spread, 0.0), axis=1, keepdims=True)
    count_rows[...] = jnp.broadcast_to(per_row, count_rows.shape)
    for copy in inputs[3:5]:
        copy.wait()
    lane = lax.broadcasted_iota(jnp.int32, (1, width), 1)
    valid = seed_count[0, 0, 0]
    marks = jnp.where(lane == block_rows, valid.astype(F32), 0.0)
    for j in range(seed_hops.shape[3]):
        marks = marks + jnp.where((lane == seed_s[0, 0, 0, j]) & (j < valid), 1.0, 0.0)
    target = labels_v[0, 0].astype(F32)
    marks = jnp.concatenate([marks[:, :labels_at], target, marks[:, labels_at + target.shape[1] :]], axis=1)
    meta_rows = pre_ref.shape[0] - rows
    slot_row = lax.broadcasted_iota(jnp.int32, (meta_rows, width), 0) == lax.axis_index("col")
    pre_ref[rows:, :] = jnp.where(slot_row, marks, 0.0).astype(BF)

    eye = jnp.where(lax.broadcasted_iota(jnp.int32, (block, block), 0) == lax.broadcasted_iota(jnp.int32, (block, block), 1), 1.0, 0.0).astype(BF)

    def chunk(k, carry):
        fetch(k).wait()

        def turn(i, carry):
            for u in range(unroll):
                at = pl.multiple_of((i * unroll + u) * block, block)
                part = stage[k, :, pl.ds(at, block)]
                if depth % 128 == 0:
                    flipped = part.T.astype(F32) if u % 4 else dot(eye, part, NT)
                else:
                    flipped = part.astype(F32).T
                rows_f32[pl.ds(pl.multiple_of(k * span + at, block), block), :] = flipped
            return carry

        lax.fori_loop(0, span // block // unroll, turn, 0)

        return carry

    lax.fori_loop(0, chunks, chunk, 0)
    inputs[2].wait()
    inputs[5].wait()
    to_scalars.wait()

    w_both = weights_v[...].reshape(2 * depth, width)

    def take(first, several):
        for b in range(several):
            b = first + b
            for r in range(block_rows):
                g, q = r // 8, r % 8
                sums[b, g, 0, q : q + 1, :] = rows_f32[pl.ds(own_s[b, 0, r], 1), :]
                total = rows_f32[pl.ds(hop_s[b, 0, 0, r], 1), :]
                for j in range(1, fan):
                    total = total + rows_f32[pl.ds(hop_s[b, j, 0, r], 1), :]
                sums[b, g, 1, q : q + 1, :] = total
        size = several * block_rows
        here = pl.ds(first * block_rows, size)
        parts_ref[here, :depth] = sums[pl.ds(first, several), :, 0].reshape(size, depth).astype(BF)
        mean = sums[pl.ds(first, several), :, 1].reshape(size, depth) / count_rows[here, :]
        parts_ref[here, depth:] = mean.astype(BF)
        pre_ref[here, :] = dot(parts_ref[here, :], w_both).astype(BF)

    several = min(groups, 4)
    if groups <= 8:
        for first in range(0, groups, several):
            take(first, several)
    else:

        @pl.loop(0, groups // several)
        def _(turn):
            take(turn * several, several)


def upper_kernel(
    batches, block_rows, labels_at, w_two, w_three, *refs
):
    *terms, hidden_ref, loss_ref, pack_ref, hidden_f32 = refs
    rows, width = pack_ref.shape[0] - 6 * batches, pack_ref.shape[1]
    me = lax.axis_index("col")
    label_count = w_three.shape[0]
    pre_one = add_up([term[:rows, :] for term in terms])
    meta = add_up([term[rows:, :] for term in terms])[:batches]
    sig_one = jax.nn.sigmoid(pre_one)
    hidden = (pre_one * sig_one).astype(BF)
    hidden_f32[...] = hidden.astype(F32)
    hidden_ref[...] = hidden_f32[pl.ds(pl.multiple_of(me * block_rows, block_rows), block_rows), :].astype(BF)
    counts = meta[:, block_rows : block_rows + 1]
    target = meta[:, labels_at : labels_at + label_count]
    batch = lax.broadcasted_iota(jnp.int32, (batches, rows), 0)
    row = lax.broadcasted_iota(jnp.int32, (batches, rows), 1)
    tiled = jnp.concatenate([meta[:, :block_rows]] * batches, axis=1)
    adjacency = jnp.where(row // block_rows == batch, tiled, 0.0)
    first = jnp.where(row == batch * block_rows, 1.0, 0.0)
    pick = jnp.concatenate([first, adjacency], axis=0).astype(BF)
    picked = dot(pick, hidden)
    seeds = picked[:batches].astype(BF)
    mean_two = (picked[batches:] / counts).astype(BF)
    w_both = w_two[...].reshape(2 * width, width)
    pre_two = dot(jnp.concatenate([seeds, mean_two], axis=1), w_both)
    sig_two = jax.nn.sigmoid(pre_two)
    hidden_two = (pre_two * sig_two).astype(BF)
    logits = dot(hidden_two, w_three[...], NT)
    soft = jnp.maximum(logits, 0.0) + jnp.log1p(jnp.exp(-jnp.abs(logits)))
    losses = jnp.mean(soft - target * logits, axis=1, keepdims=True)
    chosen = lax.broadcasted_iota(jnp.int32, losses.shape, 0) == me
    loss_ref[...] = jnp.broadcast_to(jnp.sum(jnp.where(chosen, losses, 0.0), axis=0, keepdims=True), loss_ref.shape)
    grad_logits = (jax.nn.sigmoid(logits) - target).astype(BF)
    back_two = dot(grad_logits, w_three[...])
    grad_two = (back_two * silu_slope(pre_two, sig_two)).astype(BF)
    back_both = dot(grad_two, w_both, NT)
    spread = jnp.concatenate([back_both[:, :width], back_both[:, width:] / counts], axis=0)
    pieces = []
    for _ in range(3):
        pieces.append(spread.astype(BF))
        spread = spread - pieces[-1].astype(F32)
    grad_hidden = dot(jnp.concatenate([pick] * 3, axis=0), jnp.concatenate(pieces, axis=0), TN)
    pack_ref[:rows, :] = (grad_hidden * silu_slope(pre_one, sig_one)).astype(BF)
    blank = jnp.zeros((batches, width - label_count), F32)
    tail = jnp.concatenate(
        [
            seeds.astype(F32),
            mean_two.astype(F32),
            grad_two.astype(F32),
            hidden_two.astype(F32),
            jnp.concatenate([grad_logits.astype(F32), blank], axis=1),
            jnp.zeros((batches, width), F32),
        ],
        axis=0,
    )
    pack_ref[rows:, :] = tail.astype(BF)


def products(batches, parts_t, pack):
    rows = parts_t.shape[1]

    def part(k):
        if batches % 16 == 0:
            return pack[rows + k * batches : rows + (k + 1) * batches, :]
        return pack[rows:, :].astype(F32)[k * batches : (k + 1) * batches].astype(BF)

    one = dot(parts_t, pack[:rows, :])
    return one, dot(part(0), part(2), TN), dot(part(1), part(2), TN), dot(part(4), part(3), TN)


def half_kernel(
    batches, parts_a, pack_a, parts_b, hidden, loss, one_ref, two_ref, three_ref, flipped_ref, hidden_ref, loss_ref
):
    hidden_ref[...] = hidden[...]
    loss_ref[...] = loss[:1, :1]
    one, seeds, means, three = products(batches, parts_a[...].T, pack_a)
    one_ref[...] = one
    two_ref[0] = seeds
    two_ref[1] = means
    three_ref[...] = three
    flipped_ref[...] = parts_b[...].T


def final_kernel(batches, flipped, pack_b, one_a, two_a, three_a, one_ref, two_ref, three_ref):
    depth = one_ref.shape[1]
    one, seeds, means, three = products(batches, flipped[...], pack_b)
    one = one_a[...] + one
    one_ref[0] = one[:depth]
    one_ref[1] = one[depth:]
    two_ref[0] = two_a[0] + seeds
    two_ref[1] = two_a[1] + means
    three_ref[...] = (three_a[...] + three)[: three_ref.shape[0], :]


def per_device(
    features,
    block_nodes,
    hop_two,
    hop_two_count,
    hop_one,
    hop_one_count,
    labels,
    weight_one,
    weight_two,
    weight_three,
):
    groups = lax.axis_size("col")
    depth, nodes = features.shape
    width = weight_one.shape[2]
    block_rows = block_nodes.shape[2]
    fan = hop_two.shape[2]
    label_count = weight_three.shape[1]
    rows = groups * block_rows
    meta_rows = -(-groups // 8) * 8
    labels_at = width // 2
    chunks = 16
    mib = 2**20
    row_bytes = rows * width * 4

    parts, pre = pl.pallas_call(
        functools.partial(gather_kernel, chunks, 256, 16, labels_at),
        out_shape=(
            jax.ShapeDtypeStruct((rows, 2 * depth), BF),
            jax.ShapeDtypeStruct((rows + meta_rows, width), BF),
        ),
        in_specs=[HBM] * 7 + [SMEM],
        out_specs=(VMEM, VMEM),
        scratch_shapes=[
            pltpu.VMEM((chunks, depth, nodes // chunks), BF),
            pltpu.VMEM((nodes + 8, depth), F32),
            pltpu.VMEM((groups, block_rows // 8, 2, 8, depth), F32),
            pltpu.VMEM((rows, depth), F32),
            pltpu.SMEM((groups, 1, block_rows), jnp.int32),
            pltpu.VMEM((groups, fan, 1, block_rows), jnp.int32),
            pltpu.SMEM((groups, fan, 1, block_rows), jnp.int32),
            pltpu.VMEM((groups, 1, block_rows), jnp.int32),
            pltpu.SMEM((1, 1, 1, hop_one.shape[2]), jnp.int32),
            pltpu.VMEM((1, 1, 1, label_count), jnp.int32),
            pltpu.VMEM(weight_one.shape, BF),
            pltpu.SemaphoreType.DMA((chunks,)),
            pltpu.SemaphoreType.DMA((8,)),
        ],
        compiler_params=pltpu.CompilerParams(vmem_limit_bytes=52 * mib + 2 * row_bytes),
    )(
        *(
            pltpu.with_memory_space_constraint(array, pltpu.HBM)
            for array in (
                block_nodes,
                jnp.transpose(hop_two, (0, 2, 1, 3)),
                hop_two_count,
                jnp.transpose(hop_one, (0, 1, 3, 2)),
                labels,
                weight_one,
                features,
            )
        ),
        hop_one_count,
    )

    swap = [(0, 1), (1, 0)]
    parts_b = lax.ppermute(parts, "sub", swap)
    terms = [pre]
    for number, masks in enumerate(phases(groups)):
        pre = add_up(terms).astype(BF) if number else pre
        terms = [pre] + [lax.ppermute(pre, "col", [(i, i ^ m) for i in range(groups)]) for m in masks]
        if number == 0:
            *terms, parts_b = lax.optimization_barrier((*terms, parts_b))

    hidden, loss, pack = pl.pallas_call(
        functools.partial(upper_kernel, groups, block_rows, labels_at),
        out_shape=(
            jax.ShapeDtypeStruct((block_rows, width), BF),
            jax.ShapeDtypeStruct((8, 128), F32),
            jax.ShapeDtypeStruct((rows + 6 * groups, width), BF),
        ),
        in_specs=[VMEM] * (len(terms) + 2),
        out_specs=(VMEM, VMEM, VMEM),
        scratch_shapes=[pltpu.VMEM((rows, width), F32)],
        compiler_params=pltpu.CompilerParams(vmem_limit_bytes=6 * mib + 8 * row_bytes),
    )(weight_two, weight_three.T, *terms)

    pack_b = lax.ppermute(pack, "sub", swap)
    one, two, three, flipped_b, hidden, loss = pl.pallas_call(
        functools.partial(half_kernel, groups),
        out_shape=(
            jax.ShapeDtypeStruct((2 * depth, width), F32),
            jax.ShapeDtypeStruct((2, width, width), F32),
            jax.ShapeDtypeStruct((width, width), F32),
            jax.ShapeDtypeStruct((2 * depth, rows), BF),
            jax.ShapeDtypeStruct((block_rows, width), BF),
            jax.ShapeDtypeStruct((1, 1), F32),
        ),
        in_specs=[VMEM] * 5,
        out_specs=(VMEM,) * 6,
        compiler_params=pltpu.CompilerParams(vmem_limit_bytes=6 * mib + 4 * row_bytes),
    )(parts, pack, parts_b, hidden, loss)
    grad_one, grad_two, grad_three = pl.pallas_call(
        functools.partial(final_kernel, groups),
        out_shape=(
            jax.ShapeDtypeStruct((2, depth, width), F32),
            jax.ShapeDtypeStruct((2, width, width), F32),
            jax.ShapeDtypeStruct((label_count, width), F32),
        ),
        in_specs=[VMEM] * 5,
        out_specs=(VMEM,) * 3,
        compiler_params=pltpu.CompilerParams(vmem_limit_bytes=6 * mib + 4 * row_bytes),
    )(flipped_b, pack_b, one, two, three)
    return (
        hidden.reshape(1, 1, block_rows, width),
        loss,
        grad_one,
        grad_two,
        grad_three.T,
    )


def solution(mesh):
    return jax.shard_map(
        per_device,
        mesh=mesh,
        in_specs=(
            P("col", "grp"),
            P("grp", "sub", None),
            P("grp", "sub", None, None),
            P("grp", "sub", None),
            P(("grp", "col"), "sub", None, None),
            P(("grp", "col"), "sub", None),
            P(("grp", "col"), "sub", None, None),
            P(None, "col", None),
            P(),
            P(),
        ),
        out_specs=(
            P(("grp", "col"), "sub", None, None),
            P(("grp", "col"), "sub"),
            P("grp", "col", None),
            P("grp", None, None),
            P("grp", None),
        ),
        check_vma=False,
    )
```

```python
import functools

import jax
import jax.numpy as jnp
from jax import lax
from jax.experimental import pallas as pl
from jax.experimental.pallas import tpu as pltpu
from jax.sharding import PartitionSpec as P

BF = jnp.bfloat16
F32 = jnp.float32
VMEM = pl.BlockSpec(memory_space=pltpu.VMEM)
HBM = pl.BlockSpec(memory_space=pltpu.HBM)
SMEM = pl.BlockSpec(memory_space=pltpu.SMEM)
NN = (((1,), (0,)), ((), ()))
NT = (((1,), (1,)), ((), ()))
TN = (((0,), (0,)), ((), ()))


def dot(a, b, dims=NN, **kw):
    return lax.dot_general(a, b, dims, preferred_element_type=F32, **kw)


def add_up(terms):
    terms = [term.astype(F32) for term in terms]
    while len(terms) > 1:
        terms = [a + b for a, b in zip(terms[::2], terms[1::2])]
    return terms[0]


def phases(groups):
    bits = groups.bit_length() - 1
    plan = [[1 << k, 2 << k, 3 << k] for k in range(0, bits - 1, 2)]
    if bits % 2:
        top = 1 << (bits - 1)
        plan.append([top | top >> 1])
    return plan


def silu_slope(value, sig):
    return sig * (1.0 + value * (1.0 - sig))


def gather_kernel(
    chunks, block, unroll, labels_at, own_ids, hop_ids, hop_counts, seed_hops, labels, weights, features,
    seed_count, parts_ref, pre_ref, stage, rows_f32, sums, count_rows, own_s, hop_v, hop_s, count_v, seed_s, labels_v, weights_v,
    sems, small,
):
    depth, nodes = features.shape
    span = nodes // chunks
    early = 5
    groups, _, block_rows = own_ids.shape
    fan = hop_ids.shape[1]
    rows = groups * block_rows
    width = weights.shape[2]

    def fetch(k):
        at = pl.multiple_of(k * span, span)
        return pltpu.make_async_copy(features.at[:, pl.ds(at, span)], stage.at[k], sems.at[k])

    inputs = [
        pltpu.make_async_copy(source, target, small.at[k])
        for k, (source, target) in enumerate(
            (
                (hop_ids, hop_v),
                (hop_counts, count_v),
                (own_ids, own_s),
                (seed_hops, seed_s),
                (labels, labels_v),
                (weights, weights_v),
            )
        )
    ]
    for copy in inputs[:-1]:
        copy.start()
    for k in range(early):
        fetch(k).start()
    inputs[-1].start()
    rows_f32[pl.ds(nodes, 8), :] = jnp.zeros((8, depth), F32)
    inputs[0].wait()
    inputs[1].wait()
    counts = count_v[...]
    slot_of = lax.broadcasted_iota(jnp.int32, hop_v.shape, 1)
    hop_v[...] = jnp.where(slot_of < counts[:, :, None, :], hop_v[...], nodes)
    to_scalars = pltpu.make_async_copy(hop_v, hop_s, small.at[len(inputs)])
    to_scalars.start()
    for k in range(early, chunks):
        fetch(k).start()

    member = lax.broadcasted_iota(jnp.int32, (rows, groups), 0) // block_rows
    member = jnp.where(member == lax.broadcasted_iota(jnp.int32, (rows, groups), 1), 1.0, 0.0).astype(BF)
    spread = dot(member, counts.astype(F32).reshape(groups, block_rows).astype(BF))
    here = lax.broadcasted_iota(jnp.int32, (rows, block_rows), 0) % block_rows
    here = here == lax.broadcasted_iota(jnp.int32, (rows, block_rows), 1)
    per_row = jnp.sum(jnp.where(here, spread, 0.0), axis=1, keepdims=True)
    count_rows[...] = jnp.broadcast_to(per_row, count_rows.shape)
    for copy in inputs[3:5]:
        copy.wait()
    lane = lax.broadcasted_iota(jnp.int32, (1, width), 1)
    valid = seed_count[0, 0, 0]
    marks = jnp.where(lane == block_rows, valid.astype(F32), 0.0)
    for j in range(seed_hops.shape[3]):
        marks = marks + jnp.where((lane == seed_s[0, 0, 0, j]) & (j < valid), 1.0, 0.0)
    target = labels_v[0, 0].astype(F32)
    marks = jnp.concatenate([marks[:, :labels_at], target, marks[:, labels_at + target.shape[1] :]], axis=1)
    meta_rows = pre_ref.shape[0] - rows
    slot_row = lax.broadcasted_iota(jnp.int32, (meta_rows, width), 0) == lax.axis_index("col")
    pre_ref[rows:, :] = jnp.where(slot_row, marks, 0.0).astype(BF)

    eye = jnp.where(lax.broadcasted_iota(jnp.int32, (block, block), 0) == lax.broadcasted_iota(jnp.int32, (block, block), 1), 1.0, 0.0).astype(BF)

    def chunk(k, carry):
        fetch(k).wait()

        def turn(i, carry):
            for u in range(unroll):
                at = pl.multiple_of((i * unroll + u) * block, block)
                part = stage[k, :, pl.ds(at, block)]
                if depth % 128 == 0:
                    flipped = part.T.astype(F32) if u % 4 != 1 else dot(eye, part, NT)
                else:
                    flipped = part.astype(F32).T
                rows_f32[pl.ds(pl.multiple_of(k * span + at, block), block), :] = flipped
            return carry

        lax.fori_loop(0, span // block // unroll, turn, 0)

        return carry

    lax.fori_loop(0, chunks, chunk, 0)
    inputs[2].wait()
    inputs[5].wait()
    to_scalars.wait()

    w_both = weights_v[...].reshape(2 * depth, width)

    def take(first, several):
        for b in range(several):
            b = first + b
            for r in range(block_rows):
                g, q = r // 8, r % 8
                sums[b, g, 0, q : q + 1, :] = rows_f32[pl.ds(own_s[b, 0, r], 1), :]
                total = rows_f32[pl.ds(hop_s[b, 0, 0, r], 1), :]
                for j in range(1, fan):
                    total = total + rows_f32[pl.ds(hop_s[b, j, 0, r], 1), :]
                sums[b, g, 1, q : q + 1, :] = total
        size = several * block_rows
        here = pl.ds(first * block_rows, size)
        parts_ref[here, :depth] = sums[pl.ds(first, several), :, 0].reshape(size, depth).astype(BF)
        mean = sums[pl.ds(first, several), :, 1].reshape(size, depth) / count_rows[here, :]
        parts_ref[here, depth:] = mean.astype(BF)
        pre_ref[here, :] = dot(parts_ref[here, :], w_both).astype(BF)

    several = min(groups, 4)
    if groups <= 8:
        for first in range(0, groups, several):
            take(first, several)
    else:

        @pl.loop(0, groups // several)
        def _(turn):
            take(turn * several, several)


def upper_kernel(
    batches, block_rows, labels_at, w_two, w_three, *refs
):
    *terms, hidden_ref, loss_ref, pack_ref, hidden_f32 = refs
    rows, width = pack_ref.shape[0] - 5 * batches, pack_ref.shape[1]
    me = lax.axis_index("col")
    label_count = w_three.shape[0]
    pre_one = add_up([term[:rows, :] for term in terms])
    meta = add_up([term[rows:, :] for term in terms])[:batches]
    sig_one = jax.nn.sigmoid(pre_one)
    hidden = (pre_one * sig_one).astype(BF)
    hidden_f32[...] = hidden.astype(F32)
    hidden_ref[...] = hidden_f32[pl.ds(pl.multiple_of(me * block_rows, block_rows), block_rows), :].astype(BF)
    counts = meta[:, block_rows : block_rows + 1]
    target = meta[:, labels_at : labels_at + label_count]
    batch = lax.broadcasted_iota(jnp.int32, (batches, rows), 0)
    row = lax.broadcasted_iota(jnp.int32, (batches, rows), 1)
    tiled = jnp.concatenate([meta[:, :block_rows]] * batches, axis=1)
    adjacency = jnp.where(row // block_rows == batch, tiled, 0.0)
    first = jnp.where(row == batch * block_rows, 1.0, 0.0)
    pick = jnp.concatenate([first, adjacency], axis=0).astype(BF)
    picked = dot(pick, hidden)
    seeds = picked[:batches].astype(BF)
    mean_two = (picked[batches:] / counts).astype(BF)
    w_both = w_two[...].reshape(2 * width, width)
    pre_two = dot(jnp.concatenate([seeds, mean_two], axis=1), w_both)
    sig_two = jax.nn.sigmoid(pre_two)
    hidden_two = (pre_two * sig_two).astype(BF)
    logits = dot(hidden_two, w_three[...], NT)
    soft = jnp.maximum(logits, 0.0) + jnp.log1p(jnp.exp(-jnp.abs(logits)))
    losses = jnp.mean(soft - target * logits, axis=1, keepdims=True)
    chosen = lax.broadcasted_iota(jnp.int32, losses.shape, 0) == me
    loss_ref[...] = jnp.broadcast_to(jnp.sum(jnp.where(chosen, losses, 0.0), axis=0, keepdims=True), loss_ref.shape)
    grad_logits = (jax.nn.sigmoid(logits) - target).astype(BF)
    back_two = dot(grad_logits, w_three[...])
    grad_two = (back_two * silu_slope(pre_two, sig_two)).astype(BF)
    back_both = dot(grad_two, w_both, NT)
    spread = jnp.concatenate([back_both[:, :width], back_both[:, width:] / counts], axis=0)
    pieces = []
    for _ in range(3):
        pieces.append(spread.astype(BF))
        spread = spread - pieces[-1].astype(F32)
    grad_hidden = dot(jnp.concatenate([pick] * 3, axis=0), jnp.concatenate(pieces, axis=0), TN)
    pack_ref[:rows, :] = (grad_hidden * silu_slope(pre_one, sig_one)).astype(BF)
    blank = jnp.zeros((batches, width - label_count), F32)
    tail = jnp.concatenate(
        [
            seeds.astype(F32),
            mean_two.astype(F32),
            grad_two.astype(F32),
            hidden_two.astype(F32),
            jnp.concatenate([grad_logits.astype(F32), blank], axis=1),
        ],
        axis=0,
    )
    pack_ref[rows:, :] = tail.astype(BF)


def products(batches, parts_t, pack):
    rows = parts_t.shape[1]

    def part(k):
        if batches % 16 == 0:
            return pack[rows + k * batches : rows + (k + 1) * batches, :]
        return pack[rows:, :].astype(F32)[k * batches : (k + 1) * batches].astype(BF)

    one = dot(parts_t, pack[:rows, :])
    return one, dot(part(0), part(2), TN), dot(part(1), part(2), TN), dot(part(4), part(3), TN)


def half_kernel(
    batches, parts_a, pack_a, parts_b, hidden, loss, one_ref, two_ref, three_ref, flipped_ref, hidden_ref, loss_ref
):
    hidden_ref[...] = hidden[...]
    loss_ref[...] = loss[:1, :1]
    one, seeds, means, three = products(batches, parts_a[...].T, pack_a)
    one_ref[...] = one
    two_ref[0] = seeds
    two_ref[1] = means
    three_ref[...] = three
    flipped_ref[...] = parts_b[...].T


def final_kernel(batches, flipped, pack_b, one_a, two_a, three_a, one_ref, two_ref, three_ref):
    depth = one_ref.shape[1]
    one, seeds, means, three = products(batches, flipped[...], pack_b)
    one = one_a[...] + one
    one_ref[0] = one[:depth]
    one_ref[1] = one[depth:]
    two_ref[0] = two_a[0] + seeds
    two_ref[1] = two_a[1] + means
    three_ref[...] = (three_a[...] + three)[: three_ref.shape[0], :]


def per_device(
    features,
    block_nodes,
    hop_two,
    hop_two_count,
    hop_one,
    hop_one_count,
    labels,
    weight_one,
    weight_two,
    weight_three,
):
    groups = lax.axis_size("col")
    depth, nodes = features.shape
    width = weight_one.shape[2]
    block_rows = block_nodes.shape[2]
    fan = hop_two.shape[2]
    label_count = weight_three.shape[1]
    rows = groups * block_rows
    meta_rows = -(-groups // 8) * 8
    labels_at = width // 2
    chunks = 16
    mib = 2**20
    row_bytes = rows * width * 4

    parts, pre = pl.pallas_call(
        functools.partial(gather_kernel, chunks, 256, 16, labels_at),
        out_shape=(
            jax.ShapeDtypeStruct((rows, 2 * depth), BF),
            jax.ShapeDtypeStruct((rows + meta_rows, width), BF),
        ),
        in_specs=[HBM] * 7 + [SMEM],
        out_specs=(VMEM, VMEM),
        scratch_shapes=[
            pltpu.VMEM((chunks, depth, nodes // chunks), BF),
            pltpu.VMEM((nodes + 8, depth), F32),
            pltpu.VMEM((groups, block_rows // 8, 2, 8, depth), F32),
            pltpu.VMEM((rows, depth), F32),
            pltpu.SMEM((groups, 1, block_rows), jnp.int32),
            pltpu.VMEM((groups, fan, 1, block_rows), jnp.int32),
            pltpu.SMEM((groups, fan, 1, block_rows), jnp.int32),
            pltpu.VMEM((groups, 1, block_rows), jnp.int32),
            pltpu.SMEM((1, 1, 1, hop_one.shape[2]), jnp.int32),
            pltpu.VMEM((1, 1, 1, label_count), jnp.int32),
            pltpu.VMEM(weight_one.shape, BF),
            pltpu.SemaphoreType.DMA((chunks,)),
            pltpu.SemaphoreType.DMA((8,)),
        ],
        compiler_params=pltpu.CompilerParams(vmem_limit_bytes=52 * mib + 2 * row_bytes),
    )(
        *(
            pltpu.with_memory_space_constraint(array, pltpu.HBM)
            for array in (
                block_nodes,
                jnp.transpose(hop_two, (0, 2, 1, 3)),
                hop_two_count,
                jnp.transpose(hop_one, (0, 1, 3, 2)),
                labels,
                weight_one,
                features,
            )
        ),
        hop_one_count,
    )

    swap = [(0, 1), (1, 0)]
    parts_b = lax.ppermute(parts, "sub", swap)
    terms = [pre]
    for number, masks in enumerate(phases(groups)):
        pre = add_up(terms).astype(BF) if number else pre
        terms = [pre] + [lax.ppermute(pre, "col", [(i, i ^ m) for i in range(groups)]) for m in masks]
        if number == 0:
            *terms, parts_b = lax.optimization_barrier((*terms, parts_b))

    hidden, loss, pack = pl.pallas_call(
        functools.partial(upper_kernel, groups, block_rows, labels_at),
        out_shape=(
            jax.ShapeDtypeStruct((block_rows, width), BF),
            jax.ShapeDtypeStruct((8, 128), F32),
            jax.ShapeDtypeStruct((rows + 5 * groups, width), BF),
        ),
        in_specs=[VMEM] * (len(terms) + 2),
        out_specs=(VMEM, VMEM, VMEM),
        scratch_shapes=[pltpu.VMEM((rows, width), F32)],
        compiler_params=pltpu.CompilerParams(vmem_limit_bytes=6 * mib + 8 * row_bytes),
    )(weight_two, weight_three.T, *terms)

    pack_b = lax.ppermute(pack, "sub", swap)
    one, two, three, flipped_b, hidden, loss = pl.pallas_call(
        functools.partial(half_kernel, groups),
        out_shape=(
            jax.ShapeDtypeStruct((2 * depth, width), F32),
            jax.ShapeDtypeStruct((2, width, width), F32),
            jax.ShapeDtypeStruct((width, width), F32),
            jax.ShapeDtypeStruct((2 * depth, rows), BF),
            jax.ShapeDtypeStruct((block_rows, width), BF),
            jax.ShapeDtypeStruct((1, 1), F32),
        ),
        in_specs=[VMEM] * 5,
        out_specs=(VMEM,) * 6,
        compiler_params=pltpu.CompilerParams(vmem_limit_bytes=6 * mib + 4 * row_bytes),
    )(parts, pack, parts_b, hidden, loss)
    grad_one, grad_two, grad_three = pl.pallas_call(
        functools.partial(final_kernel, groups),
        out_shape=(
            jax.ShapeDtypeStruct((2, depth, width), F32),
            jax.ShapeDtypeStruct((2, width, width), F32),
            jax.ShapeDtypeStruct((label_count, width), F32),
        ),
        in_specs=[VMEM] * 5,
        out_specs=(VMEM,) * 3,
        compiler_params=pltpu.CompilerParams(vmem_limit_bytes=6 * mib + 4 * row_bytes),
    )(flipped_b, pack_b, one, two, three)
    return (
        hidden.reshape(1, 1, block_rows, width),
        loss,
        grad_one,
        grad_two,
        grad_three.T,
    )


def solution(mesh):
    return jax.shard_map(
        per_device,
        mesh=mesh,
        in_specs=(
            P("col", "grp"),
            P("grp", "sub", None),
            P("grp", "sub", None, None),
            P("grp", "sub", None),
            P(("grp", "col"), "sub", None, None),
            P(("grp", "col"), "sub", None),
            P(("grp", "col"), "sub", None, None),
            P(None, "col", None),
            P(),
            P(),
        ),
        out_specs=(
            P(("grp", "col"), "sub", None, None),
            P(("grp", "col"), "sub"),
            P("grp", "col", None),
            P("grp", None, None),
            P("grp", None),
        ),
        check_vma=False,
    )
```
